32 devices in a mesh: row: 4 (over y, x), col: 8 (over z, core).
Axes of the slice: x: 2, y: 2, z: 4, core: 2. Of those that a mesh axis runs over, the one named last changes fastest.
Arguments:
- amplitudes: float32 [8, 24, 1, 128, 128], P('col', 'row'), may hold values from -6 to 6
- integrals: float32 [2, 512, 4096], P(None, 'row', 'col'), may hold values from -0.5 to 0.5
- owner_column: int32 [2], replicated, may hold values from 0 to 7
- occ_irrep: int32 [24], replicated, may hold values from 0 to 7, as said below
- pair_irrep: int32 [2, 4], replicated, may hold values from 0 to 7, as said below
Outputs:
- ladder: float32 [3072, 4096], P('row', 'col')
The draws below stay inside these ranges and needn't reach their ends.
Inputs may be any that keep to these rules, and one draw needn't show every extreme that they name: `occ_irrep`: every irrep 0 to 7 labels some occupied-pair tile. `pair_irrep`: in each section no irrep labels more than 1 of the 4 panel tiles, and some irrep labels exactly 1.
All inputs are finite; a program needn't handle non-finite values.
Results may differ from the reference program's by a relative error of at most 0.0001.
Values sent between devices are 32-bit elements; how exact they have to be, the bound alone decides.
No kernel may reach another device: no remote copies, remote signals or barrier semaphores. Data moves between devices by JAX's collectives and lax.ppermute only.
A program may use at most 64 MiB of HBM per device.

```python
import jax
import jax.numpy as jnp
from jax import lax

TILE = 128
IRREPS = 8
SECTIONS = 2
OCC_TILES = 24
KT = 4
CAP = 1
NVV = 4096
N_COL = 8


def draw_occ_irrep(key, part):
    label_key, place_key = jax.random.split(key)
    labels = jax.random.randint(label_key, (OCC_TILES,), 0, IRREPS, dtype=jnp.int32)
    places = jax.random.permutation(place_key, OCC_TILES)[:IRREPS]
    return labels.at[places].set(jnp.arange(IRREPS, dtype=jnp.int32))


def section_labels(key):
    busy_key, rotation_key, order_key = jax.random.split(key, 3)
    busiest = jax.random.randint(busy_key, (), 0, IRREPS, dtype=jnp.int32)
    free_turn = jax.random.randint(rotation_key, (), 0, IRREPS - 1, dtype=jnp.int32)
    rotation = jnp.where(busiest == IRREPS - 1, free_turn, IRREPS - 2 - busiest).astype(jnp.int32)
    remaining = (busiest + 1 + (jnp.arange(KT - CAP, dtype=jnp.int32) + rotation) % (IRREPS - 1)) % IRREPS
    listed = jnp.concatenate([jnp.full((CAP,), busiest, jnp.int32), remaining.astype(jnp.int32)])
    return listed[jax.random.permutation(order_key, KT)]


def draw_pair_irrep(key, part):
    return jax.vmap(section_labels)(jax.random.split(key, SECTIONS))


def shard_levels(key, shape, cuts, smallest, largest):
    level, own = 1.0, jax.random.fold_in(key, 6)
    for position, parts in cuts:
        steps = jnp.exp(jax.random.uniform(jax.random.fold_in(own, position), (parts,), jnp.float32, smallest / len(cuts), largest / len(cuts)))
        level = level * jnp.repeat(steps, shape[position] // parts).reshape([-1 if axis == position else 1 for axis in range(len(shape))])
    return level


def centred(key, shape, scale, bound, shards=(), kind=jnp.bfloat16):
    values = scale * jax.random.normal(key, shape, jnp.float32)
    if shards:
        values = values * shard_levels(key, shape, shards, -0.22, 0.18)
    return jnp.clip(values, -bound, bound).astype(kind)


def setup_inputs(seed: int = 0) -> dict:
    splits = jax.random.split(jax.random.key(seed), 6)
    amplitudes = centred(splits[0], (N_COL, OCC_TILES, CAP, TILE, TILE), 1.0, 6.0, ((0, 8), (1, 4)), jnp.float32)
    integrals = centred(splits[1], (SECTIONS, KT * TILE, NVV), (KT * TILE * SECTIONS // IRREPS) ** -0.5, 0.5, ((1, 4), (2, 8)), jnp.float32)
    owner_column = jax.random.randint(splits[2], (SECTIONS,), 0, N_COL).astype(jnp.int32)
    occ_irrep = draw_occ_irrep(jax.random.fold_in(splits[5], 71), 0)
    pair_irrep = draw_pair_irrep(jax.random.fold_in(splits[5], 71), 0)
    return dict(amplitudes=amplitudes, integrals=integrals, owner_column=owner_column, occ_irrep=occ_irrep, pair_irrep=pair_irrep)


def slot_tables(occ_labels, pair_labels):
    matches = occ_labels[:, None] == pair_labels[None, :]
    order_rank = jnp.cumsum(matches.astype(jnp.int32), axis=1) - 1
    slot_ids = jnp.arange(CAP, dtype=jnp.int32)
    chosen = matches[:, None, :] & (order_rank[:, None, :] == slot_ids[None, :, None])
    positions = jnp.arange(pair_labels.shape[0], dtype=jnp.int32)
    tile_index = jnp.sum(chosen.astype(jnp.int32) * positions[None, None, :], axis=2).astype(jnp.int32)
    valid_slot = jnp.any(chosen, axis=2)
    return tile_index, valid_slot


def reference(amplitudes, integrals, owner_column, occ_irrep, pair_irrep):
    ladder = jnp.zeros((OCC_TILES, TILE, NVV), jnp.float32)
    for which_section in range(SECTIONS):
        tile_index, valid_slot = slot_tables(occ_irrep, pair_irrep[which_section])
        amp_panel = amplitudes[owner_column[which_section]] * valid_slot[:, :, None, None].astype(jnp.float32)
        row_tiles = integrals[which_section].reshape(KT, TILE, NVV)

        def one_tile(operands):
            amp_tile, index_row = operands
            picked = jnp.take(row_tiles, index_row, axis=0)
            return jnp.einsum("sij,sjv->iv", amp_tile, picked, precision=lax.Precision.HIGHEST)

        ladder = ladder + lax.map(one_tile, (amp_panel, tile_index))
    return ladder.reshape(OCC_TILES * TILE, NVV)
```

```python
import functools

import jax
import jax.numpy as jnp
from jax import lax
from jax.experimental import pallas as pl
from jax.experimental.pallas import tpu as pltpu
from jax.sharding import PartitionSpec as P


def bits_of(count):
    assert count & (count - 1) == 0
    return [1 << place for place in range(count.bit_length() - 1)]


def swap(value, axis, size, bit):
    return lax.ppermute(value, axis, [(i, i ^ bit) for i in range(size)])


def gather_rows(block, row_size, order):
    held = {0: block}
    for bit in order:
        for offset in list(held):
            held[offset | bit] = swap(held[offset], "row", row_size, bit)
    return [held[offset] for offset in range(row_size)]


def halves(value, upper):
    middle = value.shape[1] // 2
    low, high = value[:, :middle], value[:, middle:]
    return jnp.where(upper, high, low), jnp.where(upper, low, high)


def fetch_panels(panel, owners, col_size):
    bits = bits_of(col_size)
    me = lax.axis_index("col")
    values = [panel] * len(owners)
    for bit in bits[:-1]:
        upper = (me & bit) != 0
        if bit == bits[0]:
            kept, given = halves(panel, upper)
            arrived = swap(given, "col", col_size, bit)
            pairs = [(kept, arrived)] * len(owners)
        else:
            parts = [halves(value, upper) for value in values]
            pairs = [(kept, swap(given, "col", col_size, bit)) for kept, given in parts]
        values = [
            jnp.where((owner & bit) == (me & bit), kept, arrived)
            for owner, (kept, arrived) in zip(owners, pairs)
        ]
    last = bits[-1]
    values = [
        jnp.where((owner & last) == (me & last), value, swap(value, "col", col_size, last))
        for owner, value in zip(owners, values)
    ]
    panels = []
    for value in values:
        held = {0: value}
        for place, bit in reversed(list(enumerate(bits[:-1]))):
            for offset in list(held):
                step = 1 << (len(bits) - 2 - place)
                held[offset | step] = swap(held[offset], "col", col_size, bit)
        panels.append([held[offset] for offset in range(len(held))])
    return panels


def piece_number(col_size):
    me = lax.axis_index("col")
    number = jnp.int32(0)
    for bit in bits_of(col_size)[:-1]:
        number = 2 * number + jnp.where((me & bit) != 0, 1, 0)
    return number


def slot_tables(occ_labels, pair_labels, slot_count):
    matches = occ_labels[:, None] == pair_labels[None, :]
    order_rank = jnp.cumsum(matches.astype(jnp.int32), axis=1) - 1
    slot_ids = jnp.arange(slot_count, dtype=jnp.int32)
    chosen = matches[:, None, :] & (order_rank[:, None, :] == slot_ids[None, :, None])
    positions = jnp.arange(pair_labels.shape[0], dtype=jnp.int32)
    tile_index = jnp.sum(chosen.astype(jnp.int32) * positions[None, None, :], axis=2)
    return tile_index, jnp.any(chosen, axis=2).astype(jnp.int32)


def split(value):
    high = value.astype(jnp.bfloat16)
    return high, (value - high.astype(jnp.float32)).astype(jnp.bfloat16)


def products_kernel(sections, slots, pieces, blocks, tiles, tile, columns, *refs):
    source_ref, valid_ref, piece_ref = refs[:3]
    piece_refs = refs[3 : 3 + sections * pieces]
    block_refs = refs[3 + sections * pieces : 3 + sections * (pieces + blocks)]
    out_ref, rows_high, rows_low, amp, result, sems = refs[3 + sections * (pieces + blocks) :]
    length = tile // pieces
    for k in range(sections):
        for i in range(pieces):
            start = pl.multiple_of((piece_ref[0] ^ i) * length, length)
            for o in range(tiles):
                for s in range(slots):
                    valid = valid_ref[k, o, s] != 0
                    value = jnp.where(valid, piece_refs[k * pieces + i][o, :, s * tile : (s + 1) * tile], 0.0)
                    amp[o, pl.ds(start, length), pl.ds((k * slots + s) * tile, tile)] = value
        for i in range(blocks):
            high, low = split(block_refs[k * blocks + i][...])
            rows_high[k, i] = high
            rows_low[k, i] = low

    def copy(o):
        return pltpu.make_async_copy(result.at[o], out_ref.at[pl.ds(o * tile, tile)], sems.at[o])

    for o in range(tiles):
        places = [(k, source_ref[k, o, s]) for k in range(sections) for s in range(slots)]
        high = jnp.concatenate([rows_high[k, i] for k, i in places], axis=0)
        low = jnp.concatenate([rows_low[k, i] for k, i in places], axis=0)
        dot = functools.partial(jnp.dot, preferred_element_type=jnp.float32)
        amp_high, amp_low = split(amp[o])
        result[o] = dot(amp_high, high) + (dot(amp_high, low) + dot(amp_low, high))
        copy(o).start()
    for o in range(tiles):
        copy(o).wait()


def products(source, valid, piece, panels, blocks, tiles, slots, tile):
    sections, columns = len(panels), blocks[0][0].shape[1]
    pieces, count = len(panels[0]), len(blocks[0])
    depth = sections * slots * tile
    smem = pl.BlockSpec(memory_space=pltpu.SMEM)
    vmem = pl.BlockSpec(memory_space=pltpu.VMEM)
    flat = [p for section in panels for p in section] + [b for section in blocks for b in section]
    return pl.pallas_call(
        functools.partial(products_kernel, sections, slots, pieces, count, tiles, tile, columns),
        out_shape=jax.ShapeDtypeStruct((tiles * tile, columns), jnp.float32),
        in_specs=[smem] * 3 + [vmem] * len(flat),
        out_specs=pl.BlockSpec(memory_space=pl.ANY),
        scratch_shapes=[
            pltpu.VMEM((sections, count, tile, columns), jnp.bfloat16),
            pltpu.VMEM((sections, count, tile, columns), jnp.bfloat16),
            pltpu.VMEM((tiles, tile, depth), jnp.float32),
            pltpu.VMEM((tiles, tile, columns), jnp.float32),
            pltpu.SemaphoreType.DMA((tiles,)),
        ],
        compiler_params=pltpu.CompilerParams(vmem_limit_bytes=40 * 1024 * 1024),
        cost_estimate=pl.CostEstimate(
            flops=6 * tiles * tile * depth * columns, bytes_accessed=4 * tiles * tile * columns, transcendentals=0
        ),
    )(source, valid, piece, *flat)


def on_device(row_size, col_size, amplitudes, integrals, owner_column, occ_irrep, pair_irrep):
    tiles, slots, tile = amplitudes.shape[1:4]
    sections = integrals.shape[0]
    me = lax.axis_index("row")
    occ_mine = lax.dynamic_slice_in_dim(occ_irrep, me * tiles, tiles)
    tables = [slot_tables(occ_mine, pair_irrep[k], slots) for k in range(sections)]
    source = jnp.stack([index ^ me for index, _ in tables])
    valid = jnp.stack([valid for _, valid in tables])

    order = bits_of(row_size)
    blocks = [
        gather_rows(integrals[k], row_size, order[::-1] if k % 2 == 0 else order) for k in range(sections)
    ]
    panel = amplitudes[0].transpose(0, 2, 1, 3).reshape(tiles, tile, slots * tile)
    panels = fetch_panels(panel, [owner_column[k] for k in range(sections)], col_size)
    piece = piece_number(col_size).reshape(1)
    return products(source, valid, piece, panels, blocks, tiles, slots, tile)


def solution(mesh):
    return jax.shard_map(
        functools.partial(on_device, mesh.shape["row"], mesh.shape["col"]),
        mesh=mesh,
        in_specs=(P("col", "row", None, None, None), P(None, "row", "col"), P(), P(), P()),
        out_specs=P("row", "col"),
        check_vma=False,
    )
```

```python
import functools

import jax
import jax.numpy as jnp
from jax import lax
from jax.experimental import pallas as pl
from jax.experimental.pallas import tpu as pltpu
from jax.sharding import PartitionSpec as P

SMEM = pl.BlockSpec(memory_space=pltpu.SMEM)
VMEM = pl.BlockSpec(memory_space=pltpu.VMEM)
ANY = pl.BlockSpec(memory_space=pl.ANY)
SMALL = pltpu.CompilerParams(vmem_limit_bytes=2 * 1024 * 1024)


def bits_of(count):
    assert count & (count - 1) == 0
    return [1 << place for place in range(count.bit_length() - 1)]


def swap(value, axis, size, bit):
    return lax.ppermute(value, axis, [(i, i ^ bit) for i in range(size)])


def load_kernel(slots, bits, tiles, owner_hbm, occ_hbm, pair_hbm, panel_hbm, blocks_hbm, *refs):
    sections, panel = pair_hbm.shape
    mask_ref, source_ref, piece_ref, panel_ref = refs[:4]
    block_refs, refs = refs[4 : 4 + sections], refs[4 + sections :]
    owner_ref, occ_ref, pair_ref, sems = refs
    sources = [owner_hbm, occ_hbm, pair_hbm, panel_hbm] + [blocks_hbm.at[k] for k in range(sections)]
    targets = [owner_ref, occ_ref, pair_ref, panel_ref, *block_refs]
    copies = [pltpu.make_async_copy(source, target, sems.at[i]) for i, (source, target) in enumerate(zip(sources, targets))]
    for copy in copies:
        copy.start()
    row, col = lax.axis_index("row"), lax.axis_index("col")

    def line(place, value):
        mask_ref[pl.ds(place, 1), :] = jnp.full((1, mask_ref.shape[1]), value, jnp.int32)

    for copy in copies[:3]:
        copy.wait()
    for i, bit in enumerate(bits):
        for k in range(sections):
            line(k * len(bits) + i, jnp.where((owner_ref[k] & bit) == (col & bit), 1, 0))
        line(sections * len(bits) + i, jnp.where((col & bit) != 0, 1, 0))
    for k in range(sections):
        for o in range(tiles):
            label = occ_ref[row * tiles + o]
            count = jnp.int32(0)
            chosen = [jnp.int32(-1)] * slots
            for t in range(panel):
                match = label == pair_ref[k, t]
                chosen = [
                    jnp.where(match & (count == s), row ^ t, place) for s, place in enumerate(chosen)
                ]
                count = count + jnp.where(match, 1, 0)
            for s in range(slots):
                source_ref[k, o * slots + s] = chosen[s]
    number = jnp.int32(0)
    for bit in bits[:-1]:
        number = 2 * number + jnp.where((col & bit) != 0, 1, 0)
    piece_ref[0] = number
    for copy in copies[3:]:
        copy.wait()


def load(owner, occ, pair, panel, integrals, slots, bits):
    sections, depth, columns = integrals.shape
    rows = -(-(sections + 1) * len(bits) // 8) * 8
    shape = jax.ShapeDtypeStruct
    return pl.pallas_call(
        functools.partial(load_kernel, slots, bits, panel.shape[0]),
        out_shape=(
            shape((rows, panel.shape[2]), jnp.int32),
            shape((sections, panel.shape[0] * slots), jnp.int32),
            shape((1,), jnp.int32),
            shape(panel.shape, panel.dtype),
            *[shape((depth, columns), integrals.dtype)] * sections,
        ),
        in_specs=[pl.BlockSpec(memory_space=pltpu.HBM)] * 5,
        out_specs=(VMEM, SMEM, SMEM, VMEM, *[VMEM] * sections),
        scratch_shapes=[
            pltpu.SMEM(owner.shape, jnp.int32),
            pltpu.SMEM(occ.shape, jnp.int32),
            pltpu.SMEM(pair.shape, jnp.int32),
            pltpu.SemaphoreType.DMA((4 + sections,)),
        ],
        compiler_params=pltpu.CompilerParams(vmem_limit_bytes=4 * 1024 * 1024),
    )(*[pltpu.with_memory_space_constraint(x, pltpu.HBM) for x in (owner, occ, pair, panel, integrals)])


def first_kernel(sections, rows, mine_ref, theirs_ref, mask_ref, kept_ref, given_ref):
    half, part = mine_ref.shape[1] // 2, mine_ref.shape[1] // 4
    line = lambda place: mask_ref[pl.ds(place, 1), :][None] != 0
    upper = line(sections * rows)
    cut = lambda ref: jnp.where(upper, ref[:, half:], ref[:, :half])
    mine, theirs = cut(mine_ref), cut(theirs_ref)
    high = line(sections * rows + 1)
    for k in range(sections):
        value = jnp.where(line(k * rows), mine, theirs)
        kept_ref[k] = jnp.where(high, value[:, part:], value[:, :part])
        given_ref[k] = jnp.where(high, value[:, :part], value[:, part:])


def first_choice(panel, other, masks, sections, rows):
    tiles, depth, width = panel.shape
    shape = jax.ShapeDtypeStruct((sections, tiles, depth // 4, width), panel.dtype)
    return pl.pallas_call(
        functools.partial(first_kernel, sections, rows),
        out_shape=[shape] * 2,
        in_specs=[VMEM] * 3,
        out_specs=[VMEM] * 2,
        compiler_params=SMALL,
    )(panel, other, masks)


def next_kernel(sections, rows, place, cut, mask_ref, kept_ref, arrived_ref, *refs):
    line = lambda row: mask_ref[row : row + 1, :][None] != 0
    part = kept_ref.shape[2] // 2
    for k in range(sections):
        value = jnp.where(line(k * rows + place), kept_ref[k], arrived_ref[k])
        if cut:
            high = line(sections * rows + place + 1)
            refs[-2][k] = jnp.where(high, value[:, part:], value[:, :part])
            refs[-1][k] = jnp.where(high, value[:, :part], value[:, part:])
        else:
            refs[-1][k] = value


def next_choice(kept, arrived, masks, rows, place, cut, *after):
    sections, tiles, depth, width = kept.shape
    shape = jax.ShapeDtypeStruct((sections, tiles, depth // (2 if cut else 1), width), kept.dtype)
    out = pl.pallas_call(
        functools.partial(next_kernel, sections, rows, place, cut),
        out_shape=[shape] * (2 if cut else 1),
        in_specs=[VMEM] * 3 + [ANY] * len(after),
        out_specs=[VMEM] * (2 if cut else 1),
        compiler_params=SMALL,
    )(masks, kept, arrived, *after)
    return out if cut else out[0]


def join_kernel(count, *refs):
    parts, out, at = refs[:count], refs[-1], 0
    for part in parts:
        out[at : at + part.shape[0]] = part[...]
        at += part.shape[0]


def join(parts, *after):
    count = sum(part.shape[0] for part in parts)
    return pl.pallas_call(
        functools.partial(join_kernel, len(parts)),
        out_shape=jax.ShapeDtypeStruct((count, *parts[0].shape[1:]), parts[0].dtype),
        in_specs=[VMEM] * len(parts) + [ANY] * len(after),
        out_specs=VMEM,
        compiler_params=SMALL,
    )(*parts, *after)


def split(value):
    high = value.astype(jnp.bfloat16)
    return high, (value - high.astype(jnp.float32)).astype(jnp.bfloat16)


def product(left, right):
    dot = functools.partial(jnp.dot, preferred_element_type=jnp.float32)
    (left_high, left_low), (right_high, right_low) = left, right
    return dot(left_high, right_high) + (dot(left_high, right_low) + dot(left_low, right_high))


def split_kernel(count, *refs):
    for i in range(count):
        refs[count][i], refs[count + 1][i] = split(refs[i][...])


def products_kernel(sections, blocks, sizes, source_ref, piece_ref, high, low, *refs):
    tiles, slots, tile, pieces = sizes
    part_refs, (out_ref, amp, result, sems) = refs[:-4], refs[-4:]
    length, i = tile // pieces, 0
    for part_ref in part_refs:
        for j in range(part_ref.shape[0]):
            start = pl.multiple_of((piece_ref[0] ^ i) * length, length)
            for k in range(sections):
                lanes = pl.ds(k * slots * tile, slots * tile)
                for o in range(tiles):
                    amp[o, pl.ds(start, length), lanes] = part_ref[j, k, o]
            i += 1

    def copy(o):
        return pltpu.make_async_copy(result.at[o], out_ref.at[pl.ds(o * tile, tile)], sems.at[o])

    for o in range(tiles):
        value, left, places = amp[o], [], []
        for k in range(sections):
            for s in range(slots):
                place = source_ref[k, o * slots + s]
                at = (k * slots + s) * tile
                left.append(jnp.where(place >= 0, value[:, at : at + tile], 0.0))
                places.append(k * blocks + jnp.maximum(place, 0))
        pick = lambda ref: jnp.concatenate([ref[place] for place in places], axis=0)
        result[o] = product(split(jnp.concatenate(left, axis=1)), (pick(high), pick(low)))
        copy(o).start()
    for o in range(tiles):
        copy(o).wait()


def products(source, piece, parts, blocks, sizes):
    tiles, slots, tile, pieces = sizes
    sections, count = len(blocks), len(blocks[0])
    columns, depth = blocks[0][0].shape[1], sections * slots * tile
    flat = sum(blocks, [])
    halved = jax.ShapeDtypeStruct((len(flat), tile, columns), jnp.bfloat16)
    high, low = pl.pallas_call(
        functools.partial(split_kernel, len(flat)),
        out_shape=[halved] * 2,
        in_specs=[VMEM] * len(flat),
        out_specs=[VMEM] * 2,
        compiler_params=SMALL,
    )(*flat)
    return pl.pallas_call(
        functools.partial(products_kernel, sections, count, sizes),
        out_shape=jax.ShapeDtypeStruct((tiles * tile, columns), jnp.float32),
        in_specs=[SMEM] * 2 + [VMEM] * (2 + len(parts)),
        out_specs=ANY,
        scratch_shapes=[
            pltpu.VMEM((tiles, tile, depth), jnp.float32),
            pltpu.VMEM((tiles, tile, columns), jnp.float32),
            pltpu.SemaphoreType.DMA((tiles,)),
        ],
        compiler_params=pltpu.CompilerParams(vmem_limit_bytes=16 * 1024 * 1024),
    )(source, piece, high, low, *parts)


def hold(value, *after):
    return join([value], *after)


def on_device(row_size, col_size, amplitudes, integrals, owner_column, occ_irrep, pair_irrep):
    tiles, slots, tile = amplitudes.shape[1:4]
    sections = integrals.shape[0]
    row_bits, col_bits = bits_of(row_size), bits_of(col_size)
    rows = len(col_bits)
    panel = amplitudes[0].transpose(0, 2, 1, 3).reshape(tiles, tile, slots * tile)
    along_row = lambda value, bit: swap(value, "row", row_size, bit)
    along_col = lambda value, bit: swap(value, "col", col_size, bit)

    other = along_col(panel, col_bits[0])
    first = along_row(integrals, row_bits[0])
    masks, source, piece, panel, *own = load(
        owner_column, occ_irrep, pair_irrep, panel, integrals, slots, col_bits
    )
    blocks = [{0: own[k], row_bits[0]: first[k]} for k in range(sections)]
    for k in range(sections):
        blocks[k][row_bits[-1]] = along_row(own[k], row_bits[-1])

    kept, given = first_choice(panel, other, masks, sections, rows)
    for i in range(1, rows - 1):
        cut = i < rows - 2
        out = next_choice(kept, along_col(given, col_bits[i]), masks, rows, i, cut)
        kept, given = out if cut else (out, out)
    for k in range(sections):
        for bit in row_bits[::-1] if k % 2 == 0 else row_bits:
            for offset in list(blocks[k]):
                if offset | bit not in blocks[k]:
                    blocks[k][offset | bit] = along_row(hold(blocks[k][offset], given), bit)
    blocks = [[held[offset] for offset in range(row_size)] for held in blocks]
    after = [blocks[k][row_bits[-1]] for k in range(sections)]
    parts = [next_choice(kept, along_col(given, col_bits[-1]), masks, rows, rows - 1, False, *after)[None]]
    for bit in col_bits[-2::-1]:
        held = parts[0] if len(parts) == 1 else join(parts, *[held[-1] for held in blocks])
        parts.append(along_col(held, bit))
    return products(source, piece, parts, blocks, (tiles, slots, tile, col_size // 2))


def solution(mesh):
    return jax.shard_map(
        functools.partial(on_device, mesh.shape["row"], mesh.shape["col"]),
        mesh=mesh,
        in_specs=(P("col", "row", None, None, None), P(None, "row", "col"), P(), P(), P()),
        out_specs=P("row", "col"),
        check_vma=False,
    )
```

```python
import functools

import jax
import jax.numpy as jnp
from jax import lax
from jax.experimental import pallas as pl
from jax.experimental.pallas import tpu as pltpu
from jax.sharding import PartitionSpec as P

SMEM = pl.BlockSpec(memory_space=pltpu.SMEM)
VMEM = pl.BlockSpec(memory_space=pltpu.VMEM)
ANY = pl.BlockSpec(memory_space=pl.ANY)
HBM = pl.BlockSpec(memory_space=pltpu.HBM)
SMALL = pltpu.CompilerParams(vmem_limit_bytes=4 * 1024 * 1024)


def bits_of(count):
    assert count & (count - 1) == 0
    return [1 << place for place in range(count.bit_length() - 1)]


class Sizes:
    def __init__(self, row_size, col_size, amplitudes, integrals, pair_irrep):
        self.rows, self.cols = row_size, col_size
        self.row_bits, self.col_bits = bits_of(row_size), bits_of(col_size)
        self.steps = len(self.col_bits)
        self.occ, self.slots, self.side = amplitudes.shape[1:4]
        self.tiles = self.occ * self.slots
        self.sections, self.columns = integrals.shape[0], integrals.shape[2]
        self.panel = pair_irrep.shape[1]
        self.most = self.sections * self.tiles
        shares = (8, 10, 12) if self.most <= 16 else (12,)
        self.classes = [-(-self.most * share // 12) for share in shares]
        self.own_row = self.sections * self.steps
        self.last_row = self.own_row + self.steps
        self.pair_row = self.last_row + self.steps
        self.mask_rows = -(-(self.pair_row + self.most * self.steps) // 8) * 8
        self.source_at = self.most + 1
        self.piece_at = self.source_at + self.most
        self.numbers = self.piece_at + 1


def load_kernel(z, owner_hbm, occ_hbm, pair_hbm, panel_hbm, blocks_hbm, *refs):
    mask_ref, number_ref, branch_ref, panel_ref, blocks_ref, owner_ref, occ_ref, pair_ref, sems = refs
    sources = [owner_hbm, occ_hbm, pair_hbm, panel_hbm, blocks_hbm]
    targets = [owner_ref, occ_ref, pair_ref, panel_ref, blocks_ref]
    copies = [pltpu.make_async_copy(*ends, sems.at[i]) for i, ends in enumerate(zip(sources, targets))]
    for copy in copies:
        copy.start()
    row, col = lax.axis_index("row"), lax.axis_index("col")
    one = lambda condition: jnp.where(condition, 1, 0)

    def line(place, value):
        mask_ref[pl.ds(place, 1), :] = jnp.full((1, mask_ref.shape[1]), value, jnp.int32)

    for copy in copies[:3]:
        copy.wait()

    block = []
    for t in range(z.panel):
        there, back = row ^ t, jnp.int32(0)
        for i, bit in enumerate(z.row_bits):
            back = back + jnp.where((there & bit) != 0, z.row_bits[-1 - i], 0)
        block.append(jnp.where((col & z.col_bits[0]) != 0, back, there))

    listed = jnp.int32(0)
    for k in range(z.sections):
        for o in range(z.occ):
            label = occ_ref[row * z.occ + o]
            count = jnp.int32(0)
            chosen = [jnp.int32(-1)] * z.slots
            for t in range(z.panel):
                match = label == pair_ref[k, t]
                chosen = [jnp.where(match & (count == s), block[t], place) for s, place in enumerate(chosen)]
                count = count + one(match)
            for s in range(z.slots):
                tile = k * z.tiles + o * z.slots + s
                number_ref[z.source_at + tile] = chosen[s]
                number_ref[listed] = tile
                listed = listed + one(s < count)
    for j in range(z.most + 1):
        number_ref[j] = jnp.where(listed > j, number_ref[j], z.most)
    number = jnp.int32(0)
    for bit in z.col_bits[:-1]:
        number = 2 * number + one((col & bit) != 0)
    number_ref[z.piece_at] = number

    for i, bit in enumerate(z.col_bits):
        for k in range(z.sections):
            line(k * z.steps + i, one((owner_ref[k] & bit) == (col & bit)))
        line(z.own_row + i, one((col & bit) != 0))
        line(z.last_row + i, one((owner_ref[z.sections - 1] ^ col) >> i == 0))
    for j in range(z.most):
        section = jnp.int32(0)
        for k in range(1, z.sections):
            section = section + one(number_ref[j] >= k * z.tiles)
        section = jnp.minimum(section, z.sections - 1)
        for i, bit in enumerate(z.col_bits):
            line(z.pair_row + j * z.steps + i, one((owner_ref[section] & bit) == (col & bit)))

    longest = jnp.int32(0)
    packed = []
    for k in range(z.sections):
        packed.append(jnp.int32(0))
        for t in range(z.panel):
            packed[k] = packed[k] + (jnp.int32(1) << (4 * pair_ref[k, t]))
    for r in range(z.rows):
        total = jnp.int32(0)
        for o in range(z.occ):
            shift = 4 * occ_ref[r * z.occ + o]
            for k in range(z.sections):
                total = total + ((packed[k] >> shift) & 15)
        longest = jnp.maximum(longest, total)
    differ, highest = owner_ref[0] ^ owner_ref[z.sections - 1], jnp.int32(0)
    for i in range(1, z.steps):
        highest = jnp.where(differ >> i != 0, i, highest)
    if z.sections != 2:
        highest = jnp.int32(0)
    kind = jnp.int32(0)
    for size in z.classes[:-1]:
        kind = kind + one(longest > size)
    branch_ref[0] = highest * len(z.classes) + kind
    for copy in copies[3:]:
        copy.wait()


def load(z, owner, occ, pair, panel, integrals):
    shape = jax.ShapeDtypeStruct
    arrays = [pltpu.with_memory_space_constraint(x, pltpu.HBM) for x in (owner, occ, pair, panel, integrals)]
    return pl.pallas_call(
        functools.partial(load_kernel, z),
        out_shape=(
            shape((z.mask_rows, z.side), jnp.int32),
            pltpu.SMEM((z.numbers,), jnp.int32),
            pltpu.SMEM((1,), jnp.int32),
            shape(panel.shape, panel.dtype),
            shape(integrals.shape, integrals.dtype),
        ),
        in_specs=[HBM] * 5,
        out_specs=(VMEM, SMEM, SMEM, VMEM, VMEM),
        scratch_shapes=[
            pltpu.SMEM(owner.shape, jnp.int32),
            pltpu.SMEM(occ.shape, jnp.int32),
            pltpu.SMEM(pair.shape, jnp.int32),
            pltpu.SemaphoreType.DMA((5,)),
        ],
        compiler_params=pltpu.CompilerParams(vmem_limit_bytes=8 * 1024 * 1024),
    )(*arrays)


def choose_kernel(z, step, branch, size, number_ref, mask_ref, kept_ref, arrived_ref, *refs):
    line = lambda row: mask_ref[row : row + 1, :] != 0
    further, cut = step < z.steps - 1, step < z.steps - 2 or step == 0
    outs = refs[: 2 if further and (cut or step < branch) else 1]

    def parts(value):
        if not cut:
            return value, value
        half = value.shape[-2] // 2
        low, high, upper = value[..., :half, :], value[..., half:, :], line(z.own_row + step + 1)
        return jnp.where(upper, high, low), jnp.where(upper, low, high)

    if step > branch:
        for j in range(size):
            value = jnp.where(line(z.pair_row + j * z.steps + step), kept_ref[j], arrived_ref[j])
            for out, part in zip(outs, parts(value)):
                out[j] = part
        return
    values = []
    for k in range(z.sections):
        if step == 0:
            half = z.side // 2
            side = lambda ref: jnp.where(line(z.own_row), ref[:, half:], ref[:, :half])
            mine, theirs = side(kept_ref), side(arrived_ref)
        else:
            mine, theirs = kept_ref[k], arrived_ref[0]
        values.append(jnp.where(line(k * z.steps + step), mine, theirs))
    if step < branch:
        pairs = [parts(value) for value in values]
        for k in range(z.sections):
            outs[0][k] = pairs[k][0]
        outs[1][0] = jnp.where(line(z.last_row + step + 1), pairs[-1][1], pairs[0][1])
        return
    held = refs[-1]
    for k in range(z.sections):
        held[k * z.tiles : (k + 1) * z.tiles] = values[k]
    held[z.most] = jnp.zeros(held.shape[1:], held.dtype)
    for j in range(size):
        for out, part in zip(outs, parts(held[number_ref[j]])):
            out[j] = part


def choose(z, step, branch, size, numbers, masks, kept, arrived):
    further, cut = step < z.steps - 1, step < z.steps - 2 or step == 0
    depth = z.side // 2 if step == 0 else kept.shape[-2]
    tail = (depth // 2 if cut else depth, z.side)
    shape = lambda *lead: jax.ShapeDtypeStruct((*lead, *tail), kept.dtype)
    if step < branch:
        shapes = [shape(z.sections, z.tiles), shape(1, z.tiles)]
    else:
        shapes = [shape(size)] * (2 if further and cut else 1)
    out = pl.pallas_call(
        functools.partial(choose_kernel, z, step, branch, size),
        out_shape=shapes,
        in_specs=[SMEM] + [VMEM] * 3,
        out_specs=[VMEM] * len(shapes),
        scratch_shapes=[pltpu.VMEM((z.most + 1, depth, z.side), kept.dtype)] if step == branch else [],
        compiler_params=SMALL,
    )(numbers, masks, kept, arrived)
    return out[0], out[-1]


def join_kernel(count, *refs):
    parts, out, at = refs[:count], refs[-1], 0
    for part in parts:
        out[at : at + part.shape[0]] = part[...]
        at += part.shape[0]


def join(parts, *after):
    count = sum(part.shape[0] for part in parts)
    return pl.pallas_call(
        functools.partial(join_kernel, len(parts)),
        out_shape=jax.ShapeDtypeStruct((count, *parts[0].shape[1:]), parts[0].dtype),
        in_specs=[VMEM] * len(parts) + [ANY] * len(after),
        out_specs=VMEM,
        compiler_params=SMALL,
    )(*parts, *after)


def split(value):
    high = value.astype(jnp.bfloat16)
    return high, (value - high.astype(jnp.float32)).astype(jnp.bfloat16)


def product(left, right):
    dot = functools.partial(jnp.dot, preferred_element_type=jnp.float32)
    (left_high, left_low), (right_high, right_low) = left, right
    return dot(left_high, right_high) + (dot(left_high, right_low) + dot(left_low, right_high))


def split_kernel(places, *refs):
    high, low = refs[-2:]
    for ref, at in zip(refs, places):
        for k, place in enumerate(at):
            high[place], low[place] = split(ref[k] if len(ref.shape) > 2 else ref[...])


def split_blocks(arrays, places, count, weight, earlier=()):
    tile, columns = arrays[0].shape[-2:]
    halved = jax.ShapeDtypeStruct((count, tile, columns), jnp.bfloat16)
    return pl.pallas_call(
        functools.partial(split_kernel, places),
        out_shape=[halved] * 2,
        in_specs=[VMEM] * (len(arrays) + len(earlier)),
        out_specs=[VMEM] * 2,
        input_output_aliases={len(arrays) + i: i for i in range(len(earlier))},
        compiler_params=SMALL,
        cost_estimate=pl.CostEstimate(flops=weight, bytes_accessed=1000000, transcendentals=0),
    )(*arrays, *earlier)


def products_kernel(z, size, number_ref, high, low, *refs):
    part_refs, (out_ref, amp, result, sems) = refs[:-4], refs[-4:]
    length, i = 2 * z.side // z.cols, 0
    for part_ref in part_refs:
        for p in range(part_ref.shape[0]):
            start = pl.multiple_of((number_ref[z.piece_at] ^ i) * length, length)
            for j in range(size):
                amp[number_ref[j], pl.ds(start, length), :] = part_ref[p, j]
            i += 1

    def copy(o):
        return pltpu.make_async_copy(result.at[o], out_ref.at[pl.ds(o * z.side, z.side)], sems.at[o])

    for o in range(z.occ):
        left, places = [], []
        for k in range(z.sections):
            for s in range(z.slots):
                tile = k * z.tiles + o * z.slots + s
                place = number_ref[z.source_at + tile]
                left.append(jnp.where(place >= 0, amp[tile], 0.0))
                places.append(k * z.rows + jnp.maximum(place, 0))
        pick = lambda ref: jnp.concatenate([ref[place] for place in places], axis=0)
        result[o] = product(split(jnp.concatenate(left, axis=1)), (pick(high), pick(low)))
        copy(o).start()
    for o in range(z.occ):
        copy(o).wait()


def products(z, size, numbers, high, low, parts):
    return pl.pallas_call(
        functools.partial(products_kernel, z, size),
        out_shape=pltpu.HBM((z.occ * z.side, z.columns), jnp.float32),
        in_specs=[SMEM] + [VMEM] * (2 + len(parts)),
        out_specs=ANY,
        scratch_shapes=[
            pltpu.VMEM((z.most + 1, z.side, z.side), jnp.float32),
            pltpu.VMEM((z.occ, z.side, z.columns), jnp.float32),
            pltpu.SemaphoreType.DMA((z.occ,)),
        ],
        compiler_params=pltpu.CompilerParams(vmem_limit_bytes=16 * 1024 * 1024),
    )(numbers, high, low, *parts)


def on_device(row_size, col_size, amplitudes, integrals, owner_column, occ_irrep, pair_irrep):
    z = Sizes(row_size, col_size, amplitudes, integrals, pair_irrep)
    panel = amplitudes[0].reshape(z.tiles, z.side, z.side)

    def along_col(value, bit):
        return lax.ppermute(value, "col", [(c, c ^ bit) for c in range(z.cols)])

    def along_row(value, bit):
        other = z.row_bits[-1 - z.row_bits.index(bit)]
        pairs = []
        for r in range(z.rows):
            for c in range(z.cols):
                to = r ^ (other if c & z.col_bits[0] else bit)
                pairs.append((r * z.cols + c, to * z.cols + c))
        return lax.ppermute(value, ("row", "col"), pairs)

    other = along_col(panel, z.col_bits[0])
    masks, numbers, branch, panel, own = load(z, owner_column, occ_irrep, pair_irrep, panel, integrals)

    def rest(branch, size, integrals, own, panel, other, masks, numbers):
        near, far = z.row_bits[0], z.row_bits[-1]
        wholes = {0: own, near: along_row(integrals, near), far: along_row(own, far)}
        blocks = [{i: None for i in wholes} for _ in range(z.sections)]

        kept, given = choose(z, 0, branch, size, numbers, masks, panel, other)
        for i in range(1, z.steps):
            kept, given = choose(z, i, branch, size, numbers, masks, kept, along_col(given, z.col_bits[i]))
        parts = [kept[None]]
        for bit in z.col_bits[-2::-1]:
            parts.append(along_col(parts[0] if len(parts) == 1 else join(parts), bit))

        spots = lambda i: [k * z.rows + i for k in range(z.sections)]
        high, low = split_blocks(list(wholes.values()), [spots(i) for i in wholes], z.sections * z.rows, 0)
        for k in range(z.sections)[::-1]:
            for bit in z.row_bits[::-1] if k % 2 == 0 else z.row_bits:
                for i in list(blocks[k]):
                    if i | bit not in blocks[k]:
                        value = wholes[i][k] if i in wholes else blocks[k][i]
                        blocks[k][i | bit] = along_row(value, bit)
            singles = [i for i in blocks[k] if i not in wholes]
            high, low = split_blocks(
                [blocks[k][i] for i in singles], [[k * z.rows + i] for i in singles], z.sections * z.rows,
                0, (high, low),
            )
        return products(z, size, numbers, high, low, parts)

    branches = [functools.partial(rest, h, size) for h in range(z.steps) for size in z.classes]
    return lax.switch(branch[0], branches, integrals, own, panel, other, masks, numbers)


def solution(mesh):
    return jax.shard_map(
        functools.partial(on_device, mesh.shape["row"], mesh.shape["col"]),
        mesh=mesh,
        in_specs=(P("col", "row", None, None, None), P(None, "row", "col"), P(), P(), P()),
        out_specs=P("row", "col"),
        check_vma=False,
    )
```

```python
import functools

import jax
import jax.numpy as jnp
from jax import lax
from jax.experimental import pallas as pl
from jax.experimental.pallas import tpu as pltpu
from jax.sharding import PartitionSpec as P

SMEM = pl.BlockSpec(memory_space=pltpu.SMEM)
VMEM = pl.BlockSpec(memory_space=pltpu.VMEM)
ANY = pl.BlockSpec(memory_space=pl.ANY)
HBM = pl.BlockSpec(memory_space=pltpu.HBM)
SMALL = pltpu.CompilerParams(vmem_limit_bytes=4 * 1024 * 1024)


def bits_of(count):
    assert count & (count - 1) == 0
    return [1 << place for place in range(count.bit_length() - 1)]


class Sizes:
    def __init__(self, row_size, col_size, amplitudes, integrals, pair_irrep):
        self.rows, self.cols = row_size, col_size
        self.row_bits, self.col_bits = bits_of(row_size), bits_of(col_size)
        self.steps = len(self.col_bits)
        self.occ, self.slots, self.side = amplitudes.shape[1:4]
        self.tiles = self.occ * self.slots
        self.sections, self.columns = integrals.shape[0], integrals.shape[2]
        self.panel = pair_irrep.shape[1]
        self.most = self.sections * self.tiles
        shares = (8, 10, 12) if self.most <= 16 else (12,)
        self.classes = [-(-self.most * share // 12) for share in shares]
        self.own_row = self.sections * self.steps
        self.last_row = self.own_row + self.steps
        self.pair_row = self.last_row + self.steps
        self.mask_rows = -(-(self.pair_row + self.most * self.steps) // 8) * 8
        self.source_at = self.most + 1
        self.piece_at = self.source_at + self.most
        self.numbers = self.piece_at + 1


def load_kernel(z, owner_hbm, occ_hbm, pair_hbm, panel_hbm, blocks_hbm, *refs):
    mask_ref, number_ref, branch_ref, panel_ref, blocks_ref, owner_ref, occ_ref, pair_ref, sems = refs
    sources = [owner_hbm, occ_hbm, pair_hbm, panel_hbm, blocks_hbm]
    targets = [owner_ref, occ_ref, pair_ref, panel_ref, blocks_ref]
    copies = [pltpu.make_async_copy(*ends, sems.at[i]) for i, ends in enumerate(zip(sources, targets))]
    for copy in copies:
        copy.start()
    row, col = lax.axis_index("row"), lax.axis_index("col")
    one = lambda condition: jnp.where(condition, 1, 0)

    def line(place, value):
        mask_ref[pl.ds(place, 1), :] = jnp.full((1, mask_ref.shape[1]), value, jnp.int32)

    for copy in copies[:3]:
        copy.wait()

    block = []
    for t in range(z.panel):
        there, back = row ^ t, jnp.int32(0)
        for i, bit in enumerate(z.row_bits):
            back = back + jnp.where((there & bit) != 0, z.row_bits[-1 - i], 0)
        block.append(jnp.where((col & z.col_bits[0]) != 0, back, there))

    listed = jnp.int32(0)
    for k in range(z.sections):
        for o in range(z.occ):
            label = occ_ref[row * z.occ + o]
            count = jnp.int32(0)
            chosen = [jnp.int32(-1)] * z.slots
            for t in range(z.panel):
                match = label == pair_ref[k, t]
                chosen = [jnp.where(match & (count == s), block[t], place) for s, place in enumerate(chosen)]
                count = count + one(match)
            for s in range(z.slots):
                tile = k * z.tiles + o * z.slots + s
                number_ref[z.source_at + tile] = chosen[s]
                number_ref[listed] = tile
                listed = listed + one(s < count)
    for j in range(z.most + 1):
        number_ref[j] = jnp.where(listed > j, number_ref[j], z.most)
    number = jnp.int32(0)
    for bit in z.col_bits[:-1]:
        number = 2 * number + one((col & bit) != 0)
    number_ref[z.piece_at] = number

    for i, bit in enumerate(z.col_bits):
        for k in range(z.sections):
            line(k * z.steps + i, one((owner_ref[k] & bit) == (col & bit)))
        line(z.own_row + i, one((col & bit) != 0))
        line(z.last_row + i, one((owner_ref[z.sections - 1] ^ col) >> i == 0))
    for j in range(z.most):
        section = jnp.int32(0)
        for k in range(1, z.sections):
            section = section + one(number_ref[j] >= k * z.tiles)
        section = jnp.minimum(section, z.sections - 1)
        for i, bit in enumerate(z.col_bits):
            line(z.pair_row + j * z.steps + i, one((owner_ref[section] & bit) == (col & bit)))

    longest = jnp.int32(0)
    packed = []
    for k in range(z.sections):
        packed.append(jnp.int32(0))
        for t in range(z.panel):
            packed[k] = packed[k] + (jnp.int32(1) << (4 * pair_ref[k, t]))
    for r in range(z.rows):
        total = jnp.int32(0)
        for o in range(z.occ):
            shift = 4 * occ_ref[r * z.occ + o]
            for k in range(z.sections):
                total = total + ((packed[k] >> shift) & 15)
        longest = jnp.maximum(longest, total)
    differ, highest = owner_ref[0] ^ owner_ref[z.sections - 1], jnp.int32(0)
    for i in range(1, z.steps):
        highest = jnp.where(differ >> i != 0, i, highest)
    if z.sections != 2:
        highest = jnp.int32(0)
    kind = jnp.int32(0)
    for size in z.classes[:-1]:
        kind = kind + one(longest > size)
    branch_ref[0] = highest * len(z.classes) + kind
    for copy in copies[3:]:
        copy.wait()


def load(z, owner, occ, pair, panel, integrals):
    shape = jax.ShapeDtypeStruct
    arrays = [pltpu.with_memory_space_constraint(x, pltpu.HBM) for x in (owner, occ, pair, panel, integrals)]
    return pl.pallas_call(
        functools.partial(load_kernel, z),
        out_shape=(
            shape((z.mask_rows, z.side), jnp.int32),
            pltpu.SMEM((z.numbers,), jnp.int32),
            pltpu.SMEM((1,), jnp.int32),
            shape(panel.shape, panel.dtype),
            shape(integrals.shape, integrals.dtype),
        ),
        in_specs=[HBM] * 5,
        out_specs=(VMEM, SMEM, SMEM, VMEM, VMEM),
        scratch_shapes=[
            pltpu.SMEM(owner.shape, jnp.int32),
            pltpu.SMEM(occ.shape, jnp.int32),
            pltpu.SMEM(pair.shape, jnp.int32),
            pltpu.SemaphoreType.DMA((5,)),
        ],
        compiler_params=pltpu.CompilerParams(vmem_limit_bytes=8 * 1024 * 1024),
    )(*arrays)


def choose_kernel(z, step, branch, size, number_ref, mask_ref, kept_ref, arrived_ref, *refs):
    line = lambda row: mask_ref[row : row + 1, :] != 0
    further, cut = step < z.steps - 1, step < z.steps - 2 or step == 0
    outs = refs[: 2 if further and (cut or step < branch) else 1]

    def parts(value):
        if not cut:
            return value, value
        half = value.shape[-2] // 2
        low, high, upper = value[..., :half, :], value[..., half:, :], line(z.own_row + step + 1)
        return jnp.where(upper, high, low), jnp.where(upper, low, high)

    if step > branch:
        for j in range(size):
            value = jnp.where(line(z.pair_row + j * z.steps + step), kept_ref[j], arrived_ref[j])
            for out, part in zip(outs, parts(value)):
                out[j] = part
        return
    values = []
    for k in range(z.sections):
        if step == 0:
            half = z.side // 2
            side = lambda ref: jnp.where(line(z.own_row), ref[:, half:], ref[:, :half])
            mine, theirs = side(kept_ref), side(arrived_ref)
        else:
            mine, theirs = kept_ref[k], arrived_ref[0]
        values.append(jnp.where(line(k * z.steps + step), mine, theirs))
    if step < branch:
        pairs = [parts(value) for value in values]
        for k in range(z.sections):
            outs[0][k] = pairs[k][0]
        outs[1][0] = jnp.where(line(z.last_row + step + 1), pairs[-1][1], pairs[0][1])
        return
    held = refs[-1]
    for k in range(z.sections):
        held[k * z.tiles : (k + 1) * z.tiles] = values[k]
    held[z.most] = jnp.zeros(held.shape[1:], held.dtype)
    for j in range(size):
        for out, part in zip(outs, parts(held[number_ref[j]])):
            out[j] = part


def choose(z, step, branch, size, numbers, masks, kept, arrived):
    further, cut = step < z.steps - 1, step < z.steps - 2 or step == 0
    depth = z.side // 2 if step == 0 else kept.shape[-2]
    tail = (depth // 2 if cut else depth, z.side)
    shape = lambda *lead: jax.ShapeDtypeStruct((*lead, *tail), kept.dtype)
    if step < branch:
        shapes = [shape(z.sections, z.tiles), shape(1, z.tiles)]
    else:
        shapes = [shape(size)] * (2 if further and cut else 1)
    out = pl.pallas_call(
        functools.partial(choose_kernel, z, step, branch, size),
        out_shape=shapes,
        in_specs=[SMEM] + [VMEM] * 3,
        out_specs=[VMEM] * len(shapes),
        scratch_shapes=[pltpu.VMEM((z.most + 1, depth, z.side), kept.dtype)] if step == branch else [],
        compiler_params=SMALL,
    )(numbers, masks, kept, arrived)
    return out[0], out[-1]


def join_kernel(count, *refs):
    parts, out, at = refs[:count], refs[-1], 0
    for part in parts:
        out[at : at + part.shape[0]] = part[...]
        at += part.shape[0]


def join(parts, *after):
    count = sum(part.shape[0] for part in parts)
    return pl.pallas_call(
        functools.partial(join_kernel, len(parts)),
        out_shape=jax.ShapeDtypeStruct((count, *parts[0].shape[1:]), parts[0].dtype),
        in_specs=[VMEM] * len(parts) + [ANY] * len(after),
        out_specs=VMEM,
        compiler_params=SMALL,
    )(*parts, *after)


def split(value):
    high = value.astype(jnp.bfloat16)
    return high, (value - high.astype(jnp.float32)).astype(jnp.bfloat16)


def product(left, right):
    dot = functools.partial(jnp.dot, preferred_element_type=jnp.float32)
    (left_high, left_low), (right_high, right_low) = left, right
    return dot(left_high, right_high) + (dot(left_high, right_low) + dot(left_low, right_high))


def split_kernel(places, *refs):
    high, low = refs[-2:]
    for ref, at in zip(refs, places):
        for k, place in enumerate(at):
            high[place], low[place] = split(ref[k] if len(ref.shape) > 2 else ref[...])


def split_blocks(arrays, places, count, weight, earlier=()):
    tile, columns = arrays[0].shape[-2:]
    halved = jax.ShapeDtypeStruct((count, tile, columns), jnp.bfloat16)
    return pl.pallas_call(
        functools.partial(split_kernel, places),
        out_shape=[halved] * 2,
        in_specs=[VMEM] * (len(arrays) + len(earlier)),
        out_specs=[VMEM] * 2,
        input_output_aliases={len(arrays) + i: i for i in range(len(earlier))},
        compiler_params=SMALL,
        cost_estimate=pl.CostEstimate(flops=weight, bytes_accessed=1000000, transcendentals=0),
    )(*arrays, *earlier)


def products_kernel(z, size, number_ref, high, low, *refs):
    part_refs, (out_ref, amp, result, sems) = refs[:-4], refs[-4:]
    length, i = 2 * z.side // z.cols, 0
    for part_ref in part_refs:
        for p in range(part_ref.shape[0]):
            start = pl.multiple_of((number_ref[z.piece_at] ^ i) * length, length)
            for j in range(size):
                amp[number_ref[j], pl.ds(start, length), :] = part_ref[p, j]
            i += 1

    def copy(o):
        return pltpu.make_async_copy(result.at[o], out_ref.at[pl.ds(o * z.side, z.side)], sems.at[o])

    for o in range(z.occ):
        left, places = [], []
        for k in range(z.sections):
            for s in range(z.slots):
                tile = k * z.tiles + o * z.slots + s
                place = number_ref[z.source_at + tile]
                left.append(jnp.where(place >= 0, amp[tile], 0.0))
                places.append(k * z.rows + jnp.maximum(place, 0))
        pick = lambda ref: jnp.concatenate([ref[place] for place in places], axis=0)
        result[o] = product(split(jnp.concatenate(left, axis=1)), (pick(high), pick(low)))
        copy(o).start()
    for o in range(z.occ):
        copy(o).wait()


def products(z, size, numbers, high, low, parts):
    return pl.pallas_call(
        functools.partial(products_kernel, z, size),
        out_shape=pltpu.HBM((z.occ * z.side, z.columns), jnp.float32),
        in_specs=[SMEM] + [VMEM] * (2 + len(parts)),
        out_specs=ANY,
        scratch_shapes=[
            pltpu.VMEM((z.most + 1, z.side, z.side), jnp.float32),
            pltpu.VMEM((z.occ, z.side, z.columns), jnp.float32),
            pltpu.SemaphoreType.DMA((z.occ,)),
        ],
        compiler_params=pltpu.CompilerParams(vmem_limit_bytes=16 * 1024 * 1024),
    )(numbers, high, low, *parts)


def on_device(row_size, col_size, amplitudes, integrals, owner_column, occ_irrep, pair_irrep):
    z = Sizes(row_size, col_size, amplitudes, integrals, pair_irrep)
    panel = amplitudes[0].reshape(z.tiles, z.side, z.side)

    def along_col(value, bit):
        return lax.ppermute(value, "col", [(c, c ^ bit) for c in range(z.cols)])

    def along_row(value, bit):
        other = z.row_bits[-1 - z.row_bits.index(bit)]
        pairs = []
        for r in range(z.rows):
            for c in range(z.cols):
                to = r ^ (other if c & z.col_bits[0] else bit)
                pairs.append((r * z.cols + c, to * z.cols + c))
        return lax.ppermute(value, ("row", "col"), pairs)

    other = along_col(panel, z.col_bits[0])
    masks, numbers, branch, panel, own = load(z, owner_column, occ_irrep, pair_irrep, panel, integrals)

    def rest(branch, size, integrals, own, panel, other, masks, numbers):
        near, far = z.row_bits[0], z.row_bits[-1]
        wholes = {0: own, near: along_row(integrals, near), far: along_row(own, far)}
        blocks = [{i: None for i in wholes} for _ in range(z.sections)]

        kept, given = choose(z, 0, branch, size, numbers, masks, panel, other)
        for i in range(1, z.steps):
            kept, given = choose(z, i, branch, size, numbers, masks, kept, along_col(given, z.col_bits[i]))
        parts = [kept[None]]
        for bit in z.col_bits[-2::-1]:
            parts.append(along_col(parts[0] if len(parts) == 1 else join(parts), bit))

        spots = lambda i: [k * z.rows + i for k in range(z.sections)]
        high, low = split_blocks(list(wholes.values()), [spots(i) for i in wholes], z.sections * z.rows, 0)
        for k in range(z.sections)[::-1]:
            for bit in z.row_bits[::-1] if k % 2 == 0 else z.row_bits:
                for i in list(blocks[k]):
                    if i | bit not in blocks[k]:
                        value = wholes[i][k] if i in wholes else blocks[k][i]
                        blocks[k][i | bit] = along_row(value, bit)
            singles = [i for i in blocks[k] if i not in wholes]
            high, low = split_blocks(
                [blocks[k][i] for i in singles], [[k * z.rows + i] for i in singles], z.sections * z.rows,
                2000000000, (high, low),
            )
        return products(z, size, numbers, high, low, parts)

    branches = [functools.partial(rest, h, size) for h in range(z.steps) for size in z.classes]
    return lax.switch(branch[0], branches, integrals, own, panel, other, masks, numbers)


def solution(mesh):
    return jax.shard_map(
        functools.partial(on_device, mesh.shape["row"], mesh.shape["col"]),
        mesh=mesh,
        in_specs=(P("col", "row", None, None, None), P(None, "row", "col"), P(), P(), P()),
        out_specs=P("row", "col"),
        check_vma=False,
    )
```

```python
import functools

import jax
import jax.numpy as jnp
from jax import lax
from jax.experimental import pallas as pl
from jax.experimental.pallas import tpu as pltpu
from jax.sharding import PartitionSpec as P

SMEM = pl.BlockSpec(memory_space=pltpu.SMEM)
VMEM = pl.BlockSpec(memory_space=pltpu.VMEM)
ANY = pl.BlockSpec(memory_space=pl.ANY)
HBM = pl.BlockSpec(memory_space=pltpu.HBM)
SMALL = pltpu.CompilerParams(vmem_limit_bytes=4 * 1024 * 1024)


def bits_of(count):
    assert count & (count - 1) == 0
    return [1 << place for place in range(count.bit_length() - 1)]


class Sizes:
    def __init__(self, row_size, col_size, amplitudes, integrals, pair_irrep):
        self.rows, self.cols = row_size, col_size
        self.row_bits, self.col_bits = bits_of(row_size), bits_of(col_size)
        self.steps = len(self.col_bits)
        self.occ, self.slots, self.side = amplitudes.shape[1:4]
        self.tiles = self.occ * self.slots
        self.sections, self.columns = integrals.shape[0], integrals.shape[2]
        self.panel = pair_irrep.shape[1]
        self.most = self.sections * self.tiles
        shares = (8, 10, 12) if self.most <= 16 else (12,)
        self.classes = [-(-self.most * share // 12) for share in shares]
        self.own_row = self.sections * self.steps
        self.last_row = self.own_row + self.steps
        self.pair_row = self.last_row + self.steps
        self.mask_rows = -(-(self.pair_row + self.most * self.steps) // 8) * 8
        self.source_at = self.most + 1
        self.piece_at = self.source_at + self.most
        self.numbers = self.piece_at + 1


def load_kernel(z, owner_hbm, occ_hbm, pair_hbm, panel_hbm, blocks_hbm, *refs):
    mask_ref, number_ref, branch_ref, panel_ref = refs[:4]
    block_refs, (owner_ref, occ_ref, pair_ref, sems) = refs[4:-4], refs[-4:]
    sources = [owner_hbm, occ_hbm, pair_hbm, panel_hbm] + [blocks_hbm.at[k] for k in range(z.sections)]
    targets = [owner_ref, occ_ref, pair_ref, panel_ref, *block_refs]
    copies = [pltpu.make_async_copy(*ends, sems.at[i]) for i, ends in enumerate(zip(sources, targets))]
    for copy in copies:
        copy.start()
    row, col = lax.axis_index("row"), lax.axis_index("col")
    one = lambda condition: jnp.where(condition, 1, 0)

    def line(place, value):
        mask_ref[pl.ds(place, 1), :] = jnp.full((1, mask_ref.shape[1]), value, jnp.int32)

    for copy in copies[:3]:
        copy.wait()

    block = []
    for t in range(z.panel):
        there, back = row ^ t, jnp.int32(0)
        for i, bit in enumerate(z.row_bits):
            back = back + jnp.where((there & bit) != 0, z.row_bits[-1 - i], 0)
        block.append(jnp.where((col & z.col_bits[0]) != 0, back, there))

    listed = jnp.int32(0)
    for k in range(z.sections):
        for o in range(z.occ):
            label = occ_ref[row * z.occ + o]
            count = jnp.int32(0)
            chosen = [jnp.int32(-1)] * z.slots
            for t in range(z.panel):
                match = label == pair_ref[k, t]
                chosen = [jnp.where(match & (count == s), block[t], place) for s, place in enumerate(chosen)]
                count = count + one(match)
            for s in range(z.slots):
                tile = k * z.tiles + o * z.slots + s
                number_ref[z.source_at + tile] = chosen[s]
                number_ref[listed] = tile
                listed = listed + one(s < count)
    for j in range(z.most + 1):
        number_ref[j] = jnp.where(listed > j, number_ref[j], z.most)
    number = jnp.int32(0)
    for bit in z.col_bits[:-1]:
        number = 2 * number + one((col & bit) != 0)
    number_ref[z.piece_at] = number

    longest = jnp.int32(0)
    packed = []
    for k in range(z.sections):
        packed.append(jnp.int32(0))
        for t in range(z.panel):
            packed[k] = packed[k] + (jnp.int32(1) << (4 * pair_ref[k, t]))
    for r in range(z.rows):
        total = jnp.int32(0)
        for o in range(z.occ):
            shift = 4 * occ_ref[r * z.occ + o]
            for k in range(z.sections):
                total = total + ((packed[k] >> shift) & 15)
        longest = jnp.maximum(longest, total)
    differ, highest = owner_ref[0] ^ owner_ref[z.sections - 1], jnp.int32(0)
    for i in range(1, z.steps):
        highest = jnp.where(differ >> i != 0, i, highest)
    if z.sections != 2:
        highest = jnp.int32(0)
    kind = jnp.int32(0)
    for size in z.classes[:-1]:
        kind = kind + one(longest > size)
    same = jnp.bool_(True)
    for k in range(1, z.sections):
        same = same & (owner_ref[k] == owner_ref[0])
    branch_ref[0] = jnp.where(same, z.steps * len(z.classes), highest * len(z.classes) + kind)
    for j in range(z.most):
        number_ref[j] = jnp.where(same, j if j < z.tiles else z.most, number_ref[j])
    for i, bit in enumerate(z.col_bits):
        for k in range(z.sections):
            line(k * z.steps + i, one((owner_ref[k] & bit) == (col & bit)))
        line(z.own_row + i, one((col & bit) != 0))
        line(z.last_row + i, one((owner_ref[z.sections - 1] ^ col) >> i == 0))
    for j in range(z.most):
        section = jnp.int32(0)
        for k in range(1, z.sections):
            section = section + one(number_ref[j] >= k * z.tiles)
        section = jnp.minimum(section, z.sections - 1)
        for i, bit in enumerate(z.col_bits):
            line(z.pair_row + j * z.steps + i, one((owner_ref[section] & bit) == (col & bit)))

    for copy in copies[3:]:
        copy.wait()


def load(z, owner, occ, pair, panel, integrals):
    shape = jax.ShapeDtypeStruct
    arrays = [pltpu.with_memory_space_constraint(x, pltpu.HBM) for x in (owner, occ, pair, panel, integrals)]
    return pl.pallas_call(
        functools.partial(load_kernel, z),
        out_shape=(
            shape((z.mask_rows, z.side), jnp.int32),
            pltpu.SMEM((z.numbers,), jnp.int32),
            pltpu.SMEM((1,), jnp.int32),
            shape(panel.shape, panel.dtype),
            *[shape(integrals.shape[1:], integrals.dtype)] * z.sections,
        ),
        in_specs=[HBM] * 5,
        out_specs=(VMEM, SMEM, SMEM, VMEM, *[VMEM] * z.sections),
        scratch_shapes=[
            pltpu.SMEM(owner.shape, jnp.int32),
            pltpu.SMEM(occ.shape, jnp.int32),
            pltpu.SMEM(pair.shape, jnp.int32),
            pltpu.SemaphoreType.DMA((4 + z.sections,)),
        ],
        compiler_params=pltpu.CompilerParams(vmem_limit_bytes=8 * 1024 * 1024),
    )(*arrays)


def choose_kernel(z, step, branch, size, number_ref, mask_ref, kept_ref, arrived_ref, *refs):
    line = lambda row: mask_ref[row : row + 1, :] != 0
    further, cut = step < z.steps - 1, step < z.steps - 2 or step == 0
    outs = refs[: 2 if further and (cut or step < branch) else 1]

    def parts(value):
        if not cut:
            return value, value
        half = value.shape[-2] // 2
        low, high, upper = value[..., :half, :], value[..., half:, :], line(z.own_row + step + 1)
        return jnp.where(upper, high, low), jnp.where(upper, low, high)

    if step > branch:
        for j in range(size):
            value = jnp.where(line(z.pair_row + j * z.steps + step), kept_ref[j], arrived_ref[j])
            for out, part in zip(outs, parts(value)):
                out[j] = part
        return
    values = []
    for k in range(z.sections):
        if step == 0:
            half = z.side // 2
            side = lambda ref: jnp.where(line(z.own_row), ref[:, half:], ref[:, :half])
            mine, theirs = side(kept_ref), side(arrived_ref)
        else:
            mine, theirs = kept_ref[k], arrived_ref[0]
        values.append(jnp.where(line(k * z.steps + step), mine, theirs))
    if step < branch:
        pairs = [parts(value) for value in values]
        for k in range(z.sections):
            outs[0][k] = pairs[k][0]
        outs[1][0] = jnp.where(line(z.last_row + step + 1), pairs[-1][1], pairs[0][1])
        return
    held = refs[-1]
    for k in range(z.sections):
        held[k * z.tiles : (k + 1) * z.tiles] = values[k]
    held[z.most] = jnp.zeros(held.shape[1:], held.dtype)
    for j in range(size):
        for out, part in zip(outs, parts(held[number_ref[j]])):
            out[j] = part


def choose(z, step, branch, size, numbers, masks, kept, arrived):
    further, cut = step < z.steps - 1, step < z.steps - 2 or step == 0
    depth = z.side // 2 if step == 0 else kept.shape[-2]
    tail = (depth // 2 if cut else depth, z.side)
    shape = lambda *lead: jax.ShapeDtypeStruct((*lead, *tail), kept.dtype)
    if step < branch:
        shapes = [shape(z.sections, z.tiles), shape(1, z.tiles)]
    else:
        shapes = [shape(size)] * (2 if further and cut else 1)
    out = pl.pallas_call(
        functools.partial(choose_kernel, z, step, branch, size),
        out_shape=shapes,
        in_specs=[SMEM] + [VMEM] * 3,
        out_specs=[VMEM] * len(shapes),
        scratch_shapes=[pltpu.VMEM((z.most + 1, depth, z.side), kept.dtype)] if step == branch else [],
        compiler_params=SMALL,
    )(numbers, masks, kept, arrived)
    return out[0], out[-1]


def split(value):
    high = value.astype(jnp.bfloat16)
    return high, (value - high.astype(jnp.float32)).astype(jnp.bfloat16)


def product(left, right):
    dot = functools.partial(jnp.dot, preferred_element_type=jnp.float32)
    (left_high, left_low), (right_high, right_low) = left, right
    return dot(left_high, right_high) + (dot(left_high, right_low) + dot(left_low, right_high))


def split_kernel(places, *refs):
    high, low = refs[-2:]
    for ref, at in zip(refs, places):
        for k, place in enumerate(at):
            high[place], low[place] = split(ref[k] if len(ref.shape) > 2 else ref[...])


def split_blocks(arrays, places, count, weight, earlier=()):
    tile, columns = arrays[0].shape[-2:]
    halved = jax.ShapeDtypeStruct((count, tile, columns), jnp.bfloat16)
    return pl.pallas_call(
        functools.partial(split_kernel, places),
        out_shape=[halved] * 2,
        in_specs=[VMEM] * (len(arrays) + len(earlier)),
        out_specs=[VMEM] * 2,
        input_output_aliases={len(arrays) + i: i for i in range(len(earlier))},
        compiler_params=SMALL,
        cost_estimate=pl.CostEstimate(flops=weight, bytes_accessed=1000000, transcendentals=0),
    )(*arrays, *earlier)


def products_kernel(z, size, same, number_ref, high, low, *refs):
    part_refs, (out_ref, amp, result, sems) = refs[:-4], refs[-4:]
    length = 2 * z.side // z.cols
    for i, part_ref in enumerate(part_refs):
        start = pl.multiple_of((number_ref[z.piece_at] ^ i) * length, length)
        for j in range(size):
            amp[number_ref[j], pl.ds(start, length), :] = part_ref[j]

    def copy(o):
        return pltpu.make_async_copy(result.at[o], out_ref.at[pl.ds(o * z.side, z.side)], sems.at[o])

    for o in range(z.occ):
        left, places = [], []
        for k in range(z.sections):
            for s in range(z.slots):
                tile = k * z.tiles + o * z.slots + s
                place = number_ref[z.source_at + tile]
                left.append(jnp.where(place >= 0, amp[tile % z.tiles if same else tile], 0.0))
                places.append(k * z.rows + jnp.maximum(place, 0))
        pick = lambda ref: jnp.concatenate([ref[place] for place in places], axis=0)
        result[o] = product(split(jnp.concatenate(left, axis=1)), (pick(high), pick(low)))
        copy(o).start()
    for o in range(z.occ):
        copy(o).wait()


def products(z, size, numbers, high, low, parts, same):
    return pl.pallas_call(
        functools.partial(products_kernel, z, size, same),
        out_shape=pltpu.HBM((z.occ * z.side, z.columns), jnp.float32),
        in_specs=[SMEM] + [VMEM] * (2 + len(parts)),
        out_specs=ANY,
        scratch_shapes=[
            pltpu.VMEM((z.most + 1, z.side, z.side), jnp.float32),
            pltpu.VMEM((z.occ, z.side, z.columns), jnp.float32),
            pltpu.SemaphoreType.DMA((z.occ,)),
        ],
        compiler_params=pltpu.CompilerParams(vmem_limit_bytes=16 * 1024 * 1024),
    )(numbers, high, low, *parts)


def on_device(row_size, col_size, amplitudes, integrals, owner_column, occ_irrep, pair_irrep):
    z = Sizes(row_size, col_size, amplitudes, integrals, pair_irrep)
    panel = amplitudes[0].reshape(z.tiles, z.side, z.side)

    def along_col(value, bit):
        return lax.ppermute(value, "col", [(c, c ^ bit) for c in range(z.cols)])

    def along_row(value, bit):
        other = z.row_bits[-1 - z.row_bits.index(bit)]
        pairs = []
        for r in range(z.rows):
            for c in range(z.cols):
                to = r ^ (other if c & z.col_bits[0] else bit)
                pairs.append((r * z.cols + c, to * z.cols + c))
        return lax.ppermute(value, ("row", "col"), pairs)

    other = along_col(panel, z.col_bits[0])
    masks, numbers, branch, panel, *own = load(z, owner_column, occ_irrep, pair_irrep, panel, integrals)

    def rest(branch, size, same, own, panel, other, masks, numbers):
        near, far = z.row_bits[0], z.row_bits[-1]
        blocks = [{0: own[k]} for k in range(z.sections)]
        firsts = [near if k % 2 == 0 else far for k in range(z.sections)]
        for swapped in (False, True):
            for k in range(z.sections)[:: -1 if swapped else 1]:
                bit = near + far - firsts[k] if swapped and near != far else firsts[k]
                if bit not in blocks[k]:
                    blocks[k][bit] = along_row(own[k], bit)

        kept, given = choose(z, 0, branch, size, numbers, masks, panel, other)
        for i in range(1, z.steps):
            kept, given = choose(z, i, branch, size, numbers, masks, kept, along_col(given, z.col_bits[i]))
        early = [list(held) for held in blocks]
        spot = lambda k, i: [k * z.rows + i]
        short = 3 * size <= 2 * z.most and (same or branch == z.steps - 1)
        weight = 500_000_000 if short else 1_000_000_000
        pairs = [(k, i) for k in range(z.sections) for i in early[k]]
        high, low = split_blocks(
            [blocks[k][i] for k, i in pairs], [spot(k, i) for k, i in pairs], z.sections * z.rows, 0
        )
        for k in range(z.sections):
            for bit in z.row_bits[::-1] if k % 2 == 0 else z.row_bits:
                for i in list(blocks[k]):
                    if i | bit not in blocks[k]:
                        blocks[k][i | bit] = along_row(blocks[k][i], bit)
            late = [i for i in blocks[k] if i not in early[k]]
            high, low = split_blocks(
                [blocks[k][i] for i in late], [spot(k, i) for i in late], z.sections * z.rows, weight, (high, low)
            )
        parts = [kept]
        for bit in z.col_bits[-2::-1]:
            parts += [along_col(part, bit) for part in parts]
        return products(z, size, numbers, high, low, parts, same)

    branches = [functools.partial(rest, h, size, False) for h in range(z.steps) for size in z.classes]
    branches.append(functools.partial(rest, 0, z.tiles, True))
    return lax.switch(branch[0], branches, own, panel, other, masks, numbers)


def solution(mesh):
    return jax.shard_map(
        functools.partial(on_device, mesh.shape["row"], mesh.shape["col"]),
        mesh=mesh,
        in_specs=(P("col", "row", None, None, None), P(None, "row", "col"), P(), P(), P()),
        out_specs=P("row", "col"),
        check_vma=False,
    )
```

```python
import functools

import jax
import jax.numpy as jnp
from jax import lax
from jax.experimental import pallas as pl
from jax.experimental.pallas import tpu as pltpu
from jax.sharding import PartitionSpec as P

SMEM = pl.BlockSpec(memory_space=pltpu.SMEM)
VMEM = pl.BlockSpec(memory_space=pltpu.VMEM)
ANY = pl.BlockSpec(memory_space=pl.ANY)
HBM = pl.BlockSpec(memory_space=pltpu.HBM)
SMALL = pltpu.CompilerParams(vmem_limit_bytes=4 * 1024 * 1024)


def bits_of(count):
    assert count & (count - 1) == 0
    return [1 << place for place in range(count.bit_length() - 1)]


class Sizes:
    def __init__(self, row_size, col_size, amplitudes, integrals, pair_irrep):
        self.rows, self.cols = row_size, col_size
        self.row_bits, self.col_bits = bits_of(row_size), bits_of(col_size)
        self.steps = len(self.col_bits)
        self.occ, self.slots, self.side = amplitudes.shape[1:4]
        self.tiles = self.occ * self.slots
        self.sections, self.columns = integrals.shape[0], integrals.shape[2]
        self.panel = pair_irrep.shape[1]
        self.most = self.sections * self.tiles
        shares = (8, 10, 12) if self.most <= 16 else (12,)
        self.classes = [-(-self.most * share // 12) for share in shares]
        self.own_row = self.sections * self.steps
        self.last_row = self.own_row + self.steps
        self.pair_row = self.last_row + self.steps
        self.mask_rows = -(-(self.pair_row + self.most * self.steps) // 8) * 8
        self.source_at = self.most + 1
        self.piece_at = self.source_at + self.most
        self.numbers = self.piece_at + 1


def load_kernel(z, owner_hbm, occ_hbm, pair_hbm, panel_hbm, blocks_hbm, *refs):
    mask_ref, number_ref, branch_ref, panel_ref = refs[:4]
    block_refs, (owner_ref, occ_ref, pair_ref, sems) = refs[4:-4], refs[-4:]
    sources = [owner_hbm, occ_hbm, pair_hbm, panel_hbm] + [blocks_hbm.at[k] for k in range(z.sections)]
    targets = [owner_ref, occ_ref, pair_ref, panel_ref, *block_refs]
    copies = [pltpu.make_async_copy(*ends, sems.at[i]) for i, ends in enumerate(zip(sources, targets))]
    for copy in copies:
        copy.start()
    row, col = lax.axis_index("row"), lax.axis_index("col")
    one = lambda condition: jnp.where(condition, 1, 0)

    def line(place, value):
        mask_ref[pl.ds(place, 1), :] = jnp.full((1, mask_ref.shape[1]), value, jnp.int32)

    for copy in copies[:3]:
        copy.wait()

    block = []
    for t in range(z.panel):
        there, back = row ^ t, jnp.int32(0)
        for i, bit in enumerate(z.row_bits):
            back = back + jnp.where((there & bit) != 0, z.row_bits[-1 - i], 0)
        block.append(jnp.where((col & z.col_bits[0]) != 0, back, there))

    listed = jnp.int32(0)
    for k in range(z.sections):
        for o in range(z.occ):
            label = occ_ref[row * z.occ + o]
            count = jnp.int32(0)
            chosen = [jnp.int32(-1)] * z.slots
            for t in range(z.panel):
                match = label == pair_ref[k, t]
                chosen = [jnp.where(match & (count == s), block[t], place) for s, place in enumerate(chosen)]
                count = count + one(match)
            for s in range(z.slots):
                tile = k * z.tiles + o * z.slots + s
                number_ref[z.source_at + tile] = chosen[s]
                number_ref[listed] = tile
                listed = listed + one(s < count)
    for j in range(z.most + 1):
        number_ref[j] = jnp.where(listed > j, number_ref[j], z.most)
    number = jnp.int32(0)
    for bit in z.col_bits[:-1]:
        number = 2 * number + one((col & bit) != 0)
    number_ref[z.piece_at] = number

    longest = jnp.int32(0)
    packed = []
    for k in range(z.sections):
        packed.append(jnp.int32(0))
        for t in range(z.panel):
            packed[k] = packed[k] + (jnp.int32(1) << (4 * pair_ref[k, t]))
    for r in range(z.rows):
        total = jnp.int32(0)
        for o in range(z.occ):
            shift = 4 * occ_ref[r * z.occ + o]
            for k in range(z.sections):
                total = total + ((packed[k] >> shift) & 15)
        longest = jnp.maximum(longest, total)
    differ, highest = owner_ref[0] ^ owner_ref[z.sections - 1], jnp.int32(0)
    for i in range(1, z.steps):
        highest = jnp.where(differ >> i != 0, i, highest)
    if z.sections != 2:
        highest = jnp.int32(0)
    kind = jnp.int32(0)
    for size in z.classes[:-1]:
        kind = kind + one(longest > size)
    same = jnp.bool_(True)
    for k in range(1, z.sections):
        same = same & (owner_ref[k] == owner_ref[0])
    branch_ref[0] = jnp.where(same, z.steps * len(z.classes), highest * len(z.classes) + kind)
    for j in range(z.most):
        number_ref[j] = jnp.where(same, j if j < z.tiles else z.most, number_ref[j])
    for i, bit in enumerate(z.col_bits):
        for k in range(z.sections):
            line(k * z.steps + i, one((owner_ref[k] & bit) == (col & bit)))
        line(z.own_row + i, one((col & bit) != 0))
        line(z.last_row + i, one((owner_ref[z.sections - 1] ^ col) >> i == 0))
    for j in range(z.most):
        section = jnp.int32(0)
        for k in range(1, z.sections):
            section = section + one(number_ref[j] >= k * z.tiles)
        section = jnp.minimum(section, z.sections - 1)
        for i, bit in enumerate(z.col_bits):
            line(z.pair_row + j * z.steps + i, one((owner_ref[section] & bit) == (col & bit)))

    for copy in copies[3:]:
        copy.wait()


def load(z, owner, occ, pair, panel, integrals):
    shape = jax.ShapeDtypeStruct
    arrays = [pltpu.with_memory_space_constraint(x, pltpu.HBM) for x in (owner, occ, pair, panel, integrals)]
    return pl.pallas_call(
        functools.partial(load_kernel, z),
        out_shape=(
            shape((z.mask_rows, z.side), jnp.int32),
            pltpu.SMEM((z.numbers,), jnp.int32),
            pltpu.SMEM((1,), jnp.int32),
            shape(panel.shape, panel.dtype),
            *[shape(integrals.shape[1:], integrals.dtype)] * z.sections,
        ),
        in_specs=[HBM] * 5,
        out_specs=(VMEM, SMEM, SMEM, VMEM, *[VMEM] * z.sections),
        scratch_shapes=[
            pltpu.SMEM(owner.shape, jnp.int32),
            pltpu.SMEM(occ.shape, jnp.int32),
            pltpu.SMEM(pair.shape, jnp.int32),
            pltpu.SemaphoreType.DMA((4 + z.sections,)),
        ],
        compiler_params=pltpu.CompilerParams(vmem_limit_bytes=8 * 1024 * 1024),
    )(*arrays)


def choose_kernel(z, step, branch, size, number_ref, mask_ref, kept_ref, arrived_ref, *refs):
    line = lambda row: mask_ref[row : row + 1, :] != 0
    further, cut = step < z.steps - 1, step < z.steps - 2 or step == 0
    outs = refs[: 2 if further and (cut or step < branch) else 1]

    def parts(value):
        if not cut:
            return value, value
        half = value.shape[-2] // 2
        low, high, upper = value[..., :half, :], value[..., half:, :], line(z.own_row + step + 1)
        return jnp.where(upper, high, low), jnp.where(upper, low, high)

    if step > branch:
        for j in range(size):
            value = jnp.where(line(z.pair_row + j * z.steps + step), kept_ref[j], arrived_ref[j])
            for out, part in zip(outs, parts(value)):
                out[j] = part
        return
    values = []
    for k in range(z.sections):
        if step == 0:
            half = z.side // 2
            side = lambda ref: jnp.where(line(z.own_row), ref[:, half:], ref[:, :half])
            mine, theirs = side(kept_ref), side(arrived_ref)
        else:
            mine, theirs = kept_ref[k], arrived_ref[0]
        values.append(jnp.where(line(k * z.steps + step), mine, theirs))
    if step < branch:
        pairs = [parts(value) for value in values]
        for k in range(z.sections):
            outs[0][k] = pairs[k][0]
        outs[1][0] = jnp.where(line(z.last_row + step + 1), pairs[-1][1], pairs[0][1])
        return
    held = refs[-1]
    for k in range(z.sections):
        held[k * z.tiles : (k + 1) * z.tiles] = values[k]
    held[z.most] = jnp.zeros(held.shape[1:], held.dtype)
    for j in range(size):
        for out, part in zip(outs, parts(held[number_ref[j]])):
            out[j] = part


def choose(z, step, branch, size, numbers, masks, kept, arrived):
    further, cut = step < z.steps - 1, step < z.steps - 2 or step == 0
    depth = z.side // 2 if step == 0 else kept.shape[-2]
    tail = (depth // 2 if cut else depth, z.side)
    shape = lambda *lead: jax.ShapeDtypeStruct((*lead, *tail), kept.dtype)
    if step < branch:
        shapes = [shape(z.sections, z.tiles), shape(1, z.tiles)]
    else:
        shapes = [shape(size)] * (2 if further and cut else 1)
    out = pl.pallas_call(
        functools.partial(choose_kernel, z, step, branch, size),
        out_shape=shapes,
        in_specs=[SMEM] + [VMEM] * 3,
        out_specs=[VMEM] * len(shapes),
        scratch_shapes=[pltpu.VMEM((z.most + 1, depth, z.side), kept.dtype)] if step == branch else [],
        compiler_params=SMALL,
    )(numbers, masks, kept, arrived)
    return out[0], out[-1]


def split(value):
    high = value.astype(jnp.bfloat16)
    return high, (value - high.astype(jnp.float32)).astype(jnp.bfloat16)


def product(left, right):
    dot = functools.partial(jnp.dot, preferred_element_type=jnp.float32)
    (left_high, left_low), (right_high, right_low) = left, right
    return dot(left_high, right_high) + (dot(left_high, right_low) + dot(left_low, right_high))


def split_kernel(places, *refs):
    high, low = refs[-2:]
    for ref, at in zip(refs, places):
        for k, place in enumerate(at):
            high[place], low[place] = split(ref[k] if len(ref.shape) > 2 else ref[...])


def split_blocks(arrays, places, count, weight, earlier=()):
    tile, columns = arrays[0].shape[-2:]
    halved = jax.ShapeDtypeStruct((count, tile, columns), jnp.bfloat16)
    return pl.pallas_call(
        functools.partial(split_kernel, places),
        out_shape=[halved] * 2,
        in_specs=[VMEM] * (len(arrays) + len(earlier)),
        out_specs=[VMEM] * 2,
        input_output_aliases={len(arrays) + i: i for i in range(len(earlier))},
        compiler_params=SMALL,
        cost_estimate=pl.CostEstimate(flops=weight, bytes_accessed=1000000, transcendentals=0),
    )(*arrays, *earlier)


def products_kernel(z, size, same, number_ref, high, low, *refs):
    part_refs, (out_ref, amp, result, sems) = refs[:-4], refs[-4:]
    length = 2 * z.side // z.cols
    for i, part_ref in enumerate(part_refs):
        start = pl.multiple_of((number_ref[z.piece_at] ^ i) * length, length)
        for j in range(size):
            amp[number_ref[j], pl.ds(start, length), :] = part_ref[j]

    def copy(o):
        return pltpu.make_async_copy(result.at[o], out_ref.at[pl.ds(o * z.side, z.side)], sems.at[o])

    for o in range(z.occ):
        left, places = [], []
        for k in range(z.sections):
            for s in range(z.slots):
                tile = k * z.tiles + o * z.slots + s
                place = number_ref[z.source_at + tile]
                left.append(jnp.where(place >= 0, amp[tile % z.tiles if same else tile], 0.0))
                places.append(k * z.rows + jnp.maximum(place, 0))
        pick = lambda ref: jnp.concatenate([ref[place] for place in places], axis=0)
        result[o] = product(split(jnp.concatenate(left, axis=1)), (pick(high), pick(low)))
        copy(o).start()
    for o in range(z.occ):
        copy(o).wait()


def products(z, size, numbers, high, low, parts, same):
    return pl.pallas_call(
        functools.partial(products_kernel, z, size, same),
        out_shape=pltpu.HBM((z.occ * z.side, z.columns), jnp.float32),
        in_specs=[SMEM] + [VMEM] * (2 + len(parts)),
        out_specs=ANY,
        scratch_shapes=[
            pltpu.VMEM((z.most + 1, z.side, z.side), jnp.float32),
            pltpu.VMEM((z.occ, z.side, z.columns), jnp.float32),
            pltpu.SemaphoreType.DMA((z.occ,)),
        ],
        compiler_params=pltpu.CompilerParams(vmem_limit_bytes=16 * 1024 * 1024),
    )(numbers, high, low, *parts)


def on_device(row_size, col_size, amplitudes, integrals, owner_column, occ_irrep, pair_irrep):
    z = Sizes(row_size, col_size, amplitudes, integrals, pair_irrep)
    panel = amplitudes[0].reshape(z.tiles, z.side, z.side)

    def along_col(value, bit):
        return lax.ppermute(value, "col", [(c, c ^ bit) for c in range(z.cols)])

    def along_row(value, bit):
        other = z.row_bits[-1 - z.row_bits.index(bit)]
        pairs = []
        for r in range(z.rows):
            for c in range(z.cols):
                to = r ^ (other if c & z.col_bits[0] else bit)
                pairs.append((r * z.cols + c, to * z.cols + c))
        return lax.ppermute(value, ("row", "col"), pairs)

    other = along_col(panel, z.col_bits[0])
    masks, numbers, branch, panel, *own = load(z, owner_column, occ_irrep, pair_irrep, panel, integrals)

    def rest(branch, size, same, own, panel, other, masks, numbers):
        near, far = z.row_bits[0], z.row_bits[-1]
        blocks = [{0: own[k]} for k in range(z.sections)]
        firsts = [near if k % 2 == 0 else far for k in range(z.sections)]
        for swapped in (False, True):
            for k in range(z.sections)[:: -1 if swapped else 1]:
                bit = near + far - firsts[k] if swapped and near != far else firsts[k]
                if bit not in blocks[k]:
                    blocks[k][bit] = along_row(own[k], bit)

        kept, given = choose(z, 0, branch, size, numbers, masks, panel, other)
        for i in range(1, z.steps):
            kept, given = choose(z, i, branch, size, numbers, masks, kept, along_col(given, z.col_bits[i]))
        early = [list(held) for held in blocks]
        spot = lambda k, i: [k * z.rows + i]
        short = 3 * size <= 2 * z.most and branch == z.steps - 1
        weight = 500_000_000 if short else 1_000_000_000
        pairs = [(k, i) for k in range(z.sections) for i in early[k]]
        high, low = split_blocks(
            [blocks[k][i] for k, i in pairs], [spot(k, i) for k, i in pairs], z.sections * z.rows, 0
        )
        for k in range(z.sections):
            for bit in z.row_bits[::-1] if k % 2 == 0 else z.row_bits:
                for i in list(blocks[k]):
                    if i | bit not in blocks[k]:
                        blocks[k][i | bit] = along_row(blocks[k][i], bit)
            late = [i for i in blocks[k] if i not in early[k]]
            high, low = split_blocks(
                [blocks[k][i] for i in late], [spot(k, i) for i in late], z.sections * z.rows, weight, (high, low)
            )
        parts = [kept]
        for bit in z.col_bits[-2::-1]:
            parts += [along_col(part, bit) for part in parts]
        return products(z, size, numbers, high, low, parts, same)

    branches = [functools.partial(rest, h, size, False) for h in range(z.steps) for size in z.classes]
    branches.append(functools.partial(rest, 0, z.tiles, True))
    return lax.switch(branch[0], branches, own, panel, other, masks, numbers)


def solution(mesh):
    return jax.shard_map(
        functools.partial(on_device, mesh.shape["row"], mesh.shape["col"]),
        mesh=mesh,
        in_specs=(P("col", "row", None, None, None), P(None, "row", "col"), P(), P(), P()),
        out_specs=P("row", "col"),
        check_vma=False,
    )
```

```python
import functools

import jax
import jax.numpy as jnp
from jax import lax
from jax.experimental import pallas as pl
from jax.experimental.pallas import tpu as pltpu
from jax.sharding import PartitionSpec as P

SMEM = pl.BlockSpec(memory_space=pltpu.SMEM)
VMEM = pl.BlockSpec(memory_space=pltpu.VMEM)
ANY = pl.BlockSpec(memory_space=pl.ANY)
HBM = pl.BlockSpec(memory_space=pltpu.HBM)
SMALL = pltpu.CompilerParams(vmem_limit_bytes=4 * 1024 * 1024)


def bits_of(count):
    assert count & (count - 1) == 0
    return [1 << place for place in range(count.bit_length() - 1)]


class Sizes:
    def __init__(self, row_size, col_size, amplitudes, integrals, pair_irrep):
        self.rows, self.cols = row_size, col_size
        self.row_bits, self.col_bits = bits_of(row_size), bits_of(col_size)
        self.steps = len(self.col_bits)
        self.occ, self.slots, self.side = amplitudes.shape[1:4]
        self.tiles = self.occ * self.slots
        self.sections, self.columns = integrals.shape[0], integrals.shape[2]
        self.panel = pair_irrep.shape[1]
        self.most = self.sections * self.tiles
        shares = (8, 10, 12) if self.most <= 16 else (12,)
        self.classes = [-(-self.most * share // 12) for share in shares]
        self.own_row = self.sections * self.steps
        self.last_row = self.own_row + self.steps
        self.pair_row = self.last_row + self.steps
        self.mask_rows = -(-(self.pair_row + self.most * self.steps) // 8) * 8
        self.source_at = self.most + 1
        self.piece_at = self.source_at + self.most
        self.numbers = self.piece_at + 1


def load_kernel(z, owner_hbm, occ_hbm, pair_hbm, panel_hbm, blocks_hbm, *refs):
    mask_ref, number_ref, branch_ref, panel_ref = refs[:4]
    block_refs, (owner_ref, occ_ref, pair_ref, sems) = refs[4:-4], refs[-4:]
    sources = [owner_hbm, occ_hbm, pair_hbm, panel_hbm] + [blocks_hbm.at[k] for k in range(z.sections)]
    targets = [owner_ref, occ_ref, pair_ref, panel_ref, *block_refs]
    copies = [pltpu.make_async_copy(*ends, sems.at[i]) for i, ends in enumerate(zip(sources, targets))]
    for copy in copies:
        copy.start()
    row, col = lax.axis_index("row"), lax.axis_index("col")
    one = lambda condition: jnp.where(condition, 1, 0)

    def line(place, value):
        mask_ref[pl.ds(place, 1), :] = jnp.full((1, mask_ref.shape[1]), value, jnp.int32)

    for copy in copies[:3]:
        copy.wait()

    block = []
    for t in range(z.panel):
        there, back = row ^ t, jnp.int32(0)
        for i, bit in enumerate(z.row_bits):
            back = back + jnp.where((there & bit) != 0, z.row_bits[-1 - i], 0)
        block.append(jnp.where((col & z.col_bits[0]) != 0, back, there))

    listed = jnp.int32(0)
    for k in range(z.sections):
        for o in range(z.occ):
            label = occ_ref[row * z.occ + o]
            count = jnp.int32(0)
            chosen = [jnp.int32(-1)] * z.slots
            for t in range(z.panel):
                match = label == pair_ref[k, t]
                chosen = [jnp.where(match & (count == s), block[t], place) for s, place in enumerate(chosen)]
                count = count + one(match)
            for s in range(z.slots):
                tile = k * z.tiles + o * z.slots + s
                number_ref[z.source_at + tile] = chosen[s]
                number_ref[listed] = tile
                listed = listed + one(s < count)
    for j in range(z.most + 1):
        number_ref[j] = jnp.where(listed > j, number_ref[j], z.most)
    number = jnp.int32(0)
    for bit in z.col_bits[:-1]:
        number = 2 * number + one((col & bit) != 0)
    number_ref[z.piece_at] = number

    longest = jnp.int32(0)
    packed = []
    for k in range(z.sections):
        packed.append(jnp.int32(0))
        for t in range(z.panel):
            packed[k] = packed[k] + (jnp.int32(1) << (4 * pair_ref[k, t]))
    for r in range(z.rows):
        total = jnp.int32(0)
        for o in range(z.occ):
            shift = 4 * occ_ref[r * z.occ + o]
            for k in range(z.sections):
                total = total + ((packed[k] >> shift) & 15)
        longest = jnp.maximum(longest, total)
    differ, highest = owner_ref[0] ^ owner_ref[z.sections - 1], jnp.int32(0)
    for i in range(1, z.steps):
        highest = jnp.where(differ >> i != 0, i, highest)
    if z.sections != 2:
        highest = jnp.int32(0)
    kind = jnp.int32(0)
    for size in z.classes[:-1]:
        kind = kind + one(longest > size)
    same = jnp.bool_(True)
    for k in range(1, z.sections):
        same = same & (owner_ref[k] == owner_ref[0])
    branch_ref[0] = jnp.where(same, z.steps * len(z.classes), highest * len(z.classes) + kind)
    for j in range(z.most):
        number_ref[j] = jnp.where(same, j if j < z.tiles else z.most, number_ref[j])
    for i, bit in enumerate(z.col_bits):
        for k in range(z.sections):
            line(k * z.steps + i, one((owner_ref[k] & bit) == (col & bit)))
        line(z.own_row + i, one((col & bit) != 0))
        line(z.last_row + i, one((owner_ref[z.sections - 1] ^ col) >> i == 0))
    for j in range(z.most):
        section = jnp.int32(0)
        for k in range(1, z.sections):
            section = section + one(number_ref[j] >= k * z.tiles)
        section = jnp.minimum(section, z.sections - 1)
        for i, bit in enumerate(z.col_bits):
            line(z.pair_row + j * z.steps + i, one((owner_ref[section] & bit) == (col & bit)))

    for copy in copies[3:]:
        copy.wait()


def load(z, owner, occ, pair, panel, integrals):
    shape = jax.ShapeDtypeStruct
    arrays = [pltpu.with_memory_space_constraint(x, pltpu.HBM) for x in (owner, occ, pair, panel, integrals)]
    return pl.pallas_call(
        functools.partial(load_kernel, z),
        out_shape=(
            shape((z.mask_rows, z.side), jnp.int32),
            pltpu.SMEM((z.numbers,), jnp.int32),
            pltpu.SMEM((1,), jnp.int32),
            shape(panel.shape, panel.dtype),
            *[shape(integrals.shape[1:], integrals.dtype)] * z.sections,
        ),
        in_specs=[HBM] * 5,
        out_specs=(VMEM, SMEM, SMEM, VMEM, *[VMEM] * z.sections),
        scratch_shapes=[
            pltpu.SMEM(owner.shape, jnp.int32),
            pltpu.SMEM(occ.shape, jnp.int32),
            pltpu.SMEM(pair.shape, jnp.int32),
            pltpu.SemaphoreType.DMA((4 + z.sections,)),
        ],
        compiler_params=pltpu.CompilerParams(vmem_limit_bytes=8 * 1024 * 1024),
    )(*arrays)


def choose_kernel(z, step, branch, size, number_ref, mask_ref, kept_ref, arrived_ref, *refs):
    line = lambda row: mask_ref[row : row + 1, :] != 0
    further, cut = step < z.steps - 1, step < z.steps - 2 or step == 0
    outs = refs[: 2 if further and (cut or step < branch) else 1]

    def parts(value):
        if not cut:
            return value, value
        half = value.shape[-2] // 2
        low, high, upper = value[..., :half, :], value[..., half:, :], line(z.own_row + step + 1)
        return jnp.where(upper, high, low), jnp.where(upper, low, high)

    if step > branch:
        for j in range(size):
            value = jnp.where(line(z.pair_row + j * z.steps + step), kept_ref[j], arrived_ref[j])
            for out, part in zip(outs, parts(value)):
                out[j] = part
        return
    values = []
    for k in range(z.sections):
        if step == 0:
            half = z.side // 2
            side = lambda ref: jnp.where(line(z.own_row), ref[:, half:], ref[:, :half])
            mine, theirs = side(kept_ref), side(arrived_ref)
        else:
            mine, theirs = kept_ref[k], arrived_ref[0]
        values.append(jnp.where(line(k * z.steps + step), mine, theirs))
    if step < branch:
        pairs = [parts(value) for value in values]
        for k in range(z.sections):
            outs[0][k] = pairs[k][0]
        outs[1][0] = jnp.where(line(z.last_row + step + 1), pairs[-1][1], pairs[0][1])
        return
    held = refs[-1]
    for k in range(z.sections):
        held[k * z.tiles : (k + 1) * z.tiles] = values[k]
    held[z.most] = jnp.zeros(held.shape[1:], held.dtype)
    for j in range(size):
        for out, part in zip(outs, parts(held[number_ref[j]])):
            out[j] = part


def choose(z, step, branch, size, numbers, masks, kept, arrived):
    further, cut = step < z.steps - 1, step < z.steps - 2 or step == 0
    depth = z.side // 2 if step == 0 else kept.shape[-2]
    tail = (depth // 2 if cut else depth, z.side)
    shape = lambda *lead: jax.ShapeDtypeStruct((*lead, *tail), kept.dtype)
    if step < branch:
        shapes = [shape(z.sections, z.tiles), shape(1, z.tiles)]
    else:
        shapes = [shape(size)] * (2 if further and cut else 1)
    out = pl.pallas_call(
        functools.partial(choose_kernel, z, step, branch, size),
        out_shape=shapes,
        in_specs=[SMEM] + [VMEM] * 3,
        out_specs=[VMEM] * len(shapes),
        scratch_shapes=[pltpu.VMEM((z.most + 1, depth, z.side), kept.dtype)] if step == branch else [],
        compiler_params=SMALL,
    )(numbers, masks, kept, arrived)
    return out[0], out[-1]


def split(value):
    high = value.astype(jnp.bfloat16)
    return high, (value - high.astype(jnp.float32)).astype(jnp.bfloat16)


def product(left, right):
    dot = functools.partial(jnp.dot, preferred_element_type=jnp.float32)
    (left_high, left_low), (right_high, right_low) = left, right
    return dot(left_high, right_high) + (dot(left_high, right_low) + dot(left_low, right_high))


def split_kernel(places, *refs):
    high, low = refs[-2:]
    for ref, at in zip(refs, places):
        for k, place in enumerate(at):
            high[place], low[place] = split(ref[k] if len(ref.shape) > 2 else ref[...])


def split_blocks(arrays, places, count, weight, earlier=()):
    tile, columns = arrays[0].shape[-2:]
    halved = jax.ShapeDtypeStruct((count, tile, columns), jnp.bfloat16)
    return pl.pallas_call(
        functools.partial(split_kernel, places),
        out_shape=[halved] * 2,
        in_specs=[VMEM] * (len(arrays) + len(earlier)),
        out_specs=[VMEM] * 2,
        input_output_aliases={len(arrays) + i: i for i in range(len(earlier))},
        compiler_params=SMALL,
        cost_estimate=pl.CostEstimate(flops=weight, bytes_accessed=1000000, transcendentals=0),
    )(*arrays, *earlier)


def products_kernel(z, size, same, number_ref, high, low, *refs):
    part_refs, (out_ref, amp, result, sems) = refs[:-4], refs[-4:]
    length = 2 * z.side // z.cols
    for i, part_ref in enumerate(part_refs):
        start = pl.multiple_of((number_ref[z.piece_at] ^ i) * length, length)
        for j in range(size):
            amp[number_ref[j], pl.ds(start, length), :] = part_ref[j]

    def copy(o):
        return pltpu.make_async_copy(result.at[o], out_ref.at[pl.ds(o * z.side, z.side)], sems.at[o])

    for o in range(z.occ):
        left, places = [], []
        for k in range(z.sections):
            for s in range(z.slots):
                tile = k * z.tiles + o * z.slots + s
                place = number_ref[z.source_at + tile]
                left.append(jnp.where(place >= 0, amp[tile % z.tiles if same else tile], 0.0))
                places.append(k * z.rows + jnp.maximum(place, 0))
        pick = lambda ref: jnp.concatenate([ref[place] for place in places], axis=0)
        result[o] = product(split(jnp.concatenate(left, axis=1)), (pick(high), pick(low)))
        copy(o).start()
    for o in range(z.occ):
        copy(o).wait()


def products(z, size, numbers, high, low, parts, same):
    return pl.pallas_call(
        functools.partial(products_kernel, z, size, same),
        out_shape=pltpu.HBM((z.occ * z.side, z.columns), jnp.float32),
        in_specs=[SMEM] + [VMEM] * (2 + len(parts)),
        out_specs=ANY,
        scratch_shapes=[
            pltpu.VMEM((z.most + 1, z.side, z.side), jnp.float32),
            pltpu.VMEM((z.occ, z.side, z.columns), jnp.float32),
            pltpu.SemaphoreType.DMA((z.occ,)),
        ],
        compiler_params=pltpu.CompilerParams(vmem_limit_bytes=16 * 1024 * 1024),
    )(numbers, high, low, *parts)


def on_device(row_size, col_size, amplitudes, integrals, owner_column, occ_irrep, pair_irrep):
    z = Sizes(row_size, col_size, amplitudes, integrals, pair_irrep)
    panel = amplitudes[0].reshape(z.tiles, z.side, z.side)

    def along_col(value, bit):
        return lax.ppermute(value, "col", [(c, c ^ bit) for c in range(z.cols)])

    def along_row(value, bit):
        other = z.row_bits[-1 - z.row_bits.index(bit)]
        pairs = []
        for r in range(z.rows):
            for c in range(z.cols):
                to = r ^ (other if c & z.col_bits[0] else bit)
                pairs.append((r * z.cols + c, to * z.cols + c))
        return lax.ppermute(value, ("row", "col"), pairs)

    other = along_col(panel, z.col_bits[0])
    masks, numbers, branch, panel, *own = load(z, owner_column, occ_irrep, pair_irrep, panel, integrals)

    def rest(branch, size, same, own, panel, other, masks, numbers):
        near, far = z.row_bits[0], z.row_bits[-1]
        blocks = [{0: own[k]} for k in range(z.sections)]
        firsts = [near if k % 2 == 0 else far for k in range(z.sections)]
        for swapped in (False, True):
            for k in range(z.sections)[:: -1 if swapped else 1]:
                bit = near + far - firsts[k] if swapped and near != far else firsts[k]
                if bit not in blocks[k]:
                    blocks[k][bit] = along_row(own[k], bit)

        kept, given = choose(z, 0, branch, size, numbers, masks, panel, other)
        for i in range(1, z.steps):
            kept, given = choose(z, i, branch, size, numbers, masks, kept, along_col(given, z.col_bits[i]))
        early = [list(held) for held in blocks]
        spot = lambda k, i: [k * z.rows + i]
        short, apart = 3 * size <= 2 * z.most, branch == z.steps - 1
        weight = 600_000_000 if short == apart and not same else 1_000_000_000
        weight = 500_000_000 if short and apart else weight
        pairs = [(k, i) for k in range(z.sections) for i in early[k]]
        high, low = split_blocks(
            [blocks[k][i] for k, i in pairs], [spot(k, i) for k, i in pairs], z.sections * z.rows, 0
        )
        for k in range(z.sections):
            for bit in z.row_bits[::-1] if k % 2 == 0 else z.row_bits:
                for i in list(blocks[k]):
                    if i | bit not in blocks[k]:
                        blocks[k][i | bit] = along_row(blocks[k][i], bit)
            late = [i for i in blocks[k] if i not in early[k]]
            high, low = split_blocks(
                [blocks[k][i] for i in late], [spot(k, i) for i in late], z.sections * z.rows, weight, (high, low)
            )
        parts = [kept]
        for bit in z.col_bits[-2::-1]:
            parts += [along_col(part, bit) for part in parts]
        return products(z, size, numbers, high, low, parts, same)

    branches = [functools.partial(rest, h, size, False) for h in range(z.steps) for size in z.classes]
    branches.append(functools.partial(rest, 0, z.tiles, True))
    return lax.switch(branch[0], branches, own, panel, other, masks, numbers)


def solution(mesh):
    return jax.shard_map(
        functools.partial(on_device, mesh.shape["row"], mesh.shape["col"]),
        mesh=mesh,
        in_specs=(P("col", "row", None, None, None), P(None, "row", "col"), P(), P(), P()),
        out_specs=P("row", "col"),
        check_vma=False,
    )
```
